512 devices in a mesh: box: 64 (over x, y, core), samp: 8 (over z).
Axes of the slice: x: 4, y: 8, z: 8, core: 2. Of those that a mesh axis runs over, the one named last changes fastest.
Arguments:
- fine_pattern: float32 [2, 1536, 64, 128], P(None, 'box', 'samp'), may hold values from -6 to 6
- fine_partner: int32 [1536, 16], P('box'), may hold values from 0 to 1535, as said below
- fine_offset: int32 [1536, 16], P('box'), may hold values from 0 to 15
- fine_count: int32 [1536], P('box'), may hold values from 1 to 16, as said below
- coarse_partner: int32 [192, 16], P('box'), may hold values from 0 to 191, as said below
- coarse_offset: int32 [192, 16], P('box'), may hold values from 0 to 15
- coarse_count: int32 [192], P('box'), may hold values from 1 to 16, as said below
- fine_table: float32 [2, 16, 64, 128], P(None, None, 'samp'), may hold values from -1.5 to 1.5
- coarse_table: float32 [2, 16, 128, 256], P(None, None, 'samp'), may hold values from -1.5 to 1.5
- theta_start: int32 [128], P('samp'), may hold values from 0 to 60, as said below
- theta_weight: float32 [128, 4], P('samp'), may hold values from -0.5 to 1
- phi_interp: float32 [256, 128], replicated, may hold values from -0.1875 to 0.1875
- shift_phase: float32 [8, 128, 256], P(None, 'samp'), may hold values from -3.140625 to 3.140625
Outputs:
- fine_incoming: float32 [2, 1536, 64, 128], P(None, 'box', 'samp')
- coarse_incoming: float32 [2, 192, 128, 256], P(None, 'box', 'samp')
The draws below stay inside these ranges and needn't reach their ends.
Inputs may be any that keep to these rules, and one draw needn't show every extreme that they name: `fine_partner`: partners of a box on box index d lie on box indices d - 1 to d + 1, are distinct, never the box itself or the boxes next to it in order; some box on each inner index has partners on both ends of that range. Slots at and after the box's count hold the box itself. `fine_count`: counts are limited by the boxes available in the range above. `coarse_partner`: partners of a box on box index d lie on box indices d - 4 to d + 4, are distinct, never the box itself or the boxes next to it in order; some box on each inner index has partners on both ends of that range. Slots at and after the box's count hold the box itself. `coarse_count`: counts are limited by the boxes available in the range above. `theta_start`: for upper-level row i, the start lies between floor(i / 2) - 2 and floor(i / 2) - 1, clamped to the grid.
All inputs are finite; a program needn't handle non-finite values.
Results may differ from the reference program's by a relative error of at most 0.00007.
Values sent between devices are 32-bit elements; how exact they have to be, the bound alone decides.
No kernel may reach another device: no remote copies, remote signals or barrier semaphores. Data moves between devices by JAX's collectives and lax.ppermute only.
A program may use at most 64 MiB of HBM per device.

```python
import jax
import jax.numpy as jnp
from jax import lax

T1 = 64
P1 = 128
T2 = 128
P2 = 256
NOFF = 16
PMAX = 16
B1_DEV = 24
B2_DEV = 3
NB1 = 1536
NB2 = 192
REACH1 = 1
REACH2 = 4
N_SAMP = 8


def window_lists(key, boxes_dev, reach, total):
    rows = jnp.arange(total, dtype=jnp.int32)
    device = rows // boxes_dev
    width = (2 * reach + 1) * boxes_dev
    spots = jnp.arange(width, dtype=jnp.int32)
    first = (device - reach) * boxes_dev
    candidate = first[:, None] + spots[None, :]
    valid = (candidate >= 0) & (candidate < total) & (jnp.abs(candidate - rows[:, None]) > 1)
    key_score, key_count = jax.random.split(key)
    random_part = jax.random.randint(key_score, (total, width), 1, 2 ** 20, dtype=jnp.int32)
    score = jnp.where(valid, random_part * width + spots[None, :], -1 - spots[None, :])
    ends = (spots == 0) | (spots == width - 1)
    score = jnp.where(valid & ends[None, :], 2 ** 30 + spots[None, :], score)
    top_values, picks = lax.top_k(score, PMAX)
    partner = first[:, None] + picks.astype(jnp.int32)
    available = jnp.sum(valid.astype(jnp.int32), axis=1)
    count = PMAX - jax.random.randint(key_count, (total,), 0, PMAX // 3 + 1, dtype=jnp.int32)
    count = jnp.where(rows % 3 == 0, PMAX, count)
    count = jnp.minimum(count, available).astype(jnp.int32)
    slots = jnp.arange(PMAX, dtype=jnp.int32)
    partner = jnp.where(slots[None, :] < count[:, None], partner, rows[:, None])
    return (partner.astype(jnp.int32), count)


def draw_fine_partner(key, part):
    partner, count = window_lists(jax.random.fold_in(key, 11), B1_DEV, REACH1, NB1)
    return partner


def draw_fine_count(key, part):
    partner, count = window_lists(jax.random.fold_in(key, 11), B1_DEV, REACH1, NB1)
    return count


def draw_coarse_partner(key, part):
    partner, count = window_lists(jax.random.fold_in(key, 12), B2_DEV, REACH2, NB2)
    return partner


def draw_coarse_count(key, part):
    partner, count = window_lists(jax.random.fold_in(key, 12), B2_DEV, REACH2, NB2)
    return count


def draw_theta_start(key, part):
    key = jax.random.fold_in(key, 5)
    rows = jnp.arange(T2, dtype=jnp.int32)
    block = T2 // N_SAMP
    jitter = jax.random.randint(key, (T2,), 0, 2, dtype=jnp.int32)
    jitter = jnp.where(rows % block == 0, 1, jitter)
    jitter = jnp.where(rows % block == block - 1, 0, jitter)
    return jnp.clip(rows // 2 - 1 - jitter, 0, T1 - 4).astype(jnp.int32)


def plant(array, stream_key, smallest, top_value):
    place = [jax.random.randint(jax.random.fold_in(stream_key, axis), (), 0, length) for axis, length in enumerate(array.shape)]
    widest = array.shape.index(max(array.shape))
    beside = place[:widest] + [(place[widest] + 1) % array.shape[widest]] + place[widest + 1:]
    return array.at[tuple(place)].set(smallest).at[tuple(beside)].set(top_value)


def shard_levels(own_key, extent, cuts, least, high):
    def one(position, parts):
        draws = jax.random.uniform(jax.random.fold_in(jax.random.fold_in(own_key, 6), position), (parts,), jnp.float32, least / len(cuts), high / len(cuts))
        return jnp.repeat(jnp.exp(draws), extent[position] // parts).reshape((-1,) + (1,) * (len(extent) - position - 1))

    factor_of = one(*cuts[0])
    for cut in cuts[1:]:
        factor_of = factor_of * one(*cut)
    return factor_of


def centred(key, shape, scale, most, shards=(), held_as=jnp.bfloat16):
    factor_of = shard_levels(key, shape, shards, -0.22, 0.18) if shards else 1.0
    values = jax.random.normal(key, shape, jnp.float32) * scale * factor_of
    return jnp.minimum(jnp.maximum(values, -most), most).astype(held_as)


def setup_inputs(seed: int = 0) -> dict:
    key_of = jax.random.split(jax.random.key(seed), 14)
    return {
        "fine_pattern": centred(key_of[0], (2, NB1, T1, P1), 1.0, 6.0, ((1, 64), (2, 8)), jnp.float32),
        "fine_partner": draw_fine_partner(jax.random.fold_in(key_of[13], 71), 0),
        "fine_offset": plant(jax.random.randint(key_of[2], (NB1, PMAX), 0, NOFF), jax.random.fold_in(key_of[2], 1), 0, NOFF - 1).astype(jnp.int32),
        "fine_count": draw_fine_count(jax.random.fold_in(key_of[13], 71), 0),
        "coarse_partner": draw_coarse_partner(jax.random.fold_in(key_of[13], 71), 0),
        "coarse_offset": plant(jax.random.randint(key_of[5], (NB2, PMAX), 0, NOFF), jax.random.fold_in(key_of[5], 1), 0, NOFF - 1).astype(jnp.int32),
        "coarse_count": draw_coarse_count(jax.random.fold_in(key_of[13], 71), 0),
        "fine_table": centred(key_of[7], (2, NOFF, T1, P1), PMAX ** -0.5, 1.5, ((2, 8),), jnp.float32),
        "coarse_table": centred(key_of[8], (2, NOFF, T2, P2), PMAX ** -0.5, 1.5, ((2, 8),), jnp.float32),
        "theta_start": draw_theta_start(jax.random.fold_in(key_of[13], 71), 0),
        "theta_weight": jnp.clip(-0.5 + 1.5 * jax.random.uniform(key_of[10], (T2, 4), jnp.float32) ** shard_levels(key_of[10], (T2, 4), ((0, 8),), -0.2, 0.2), -0.5, 1.0),
        "phi_interp": centred(key_of[11], (P2, P1), (8 * P1) ** -0.5, 0.1875, (), jnp.float32),
        "shift_phase": jnp.clip(jax.random.uniform(key_of[12], (8, T2, P2), jnp.float32, -3.140625, 3.140625), -3.140625, 3.140625),
    }


def translate(pattern, table, partner, offset, count):
    start = jnp.zeros((2, partner.shape[0]) + pattern.shape[2:], jnp.float32)

    def step(slot, total):
        source = pattern[:, partner[:, slot]]
        operator = table[:, offset[:, slot]]
        alive = (slot < count).astype(jnp.float32)[:, None, None]
        real_part = (operator[0] * source[0] - operator[1] * source[1]) * alive
        imag_part = (operator[0] * source[1] + operator[1] * source[0]) * alive
        return total + jnp.stack([real_part, imag_part])

    return lax.fori_loop(0, partner.shape[1], step, start)


def aggregate(source, start_row, theta_weight, phi_interp, shift_phase):
    grid = jnp.arange(source.shape[2], dtype=jnp.int32)
    stencil = start_row[:, None] + jnp.arange(4, dtype=jnp.int32)[None, :]
    picked = (stencil[:, :, None] == grid[None, None, :]).astype(jnp.float32)
    theta_matrix = jnp.sum(theta_weight[:, :, None] * picked, axis=1)
    narrow = jnp.einsum("xbrp,ir->xbip", source, theta_matrix, precision=lax.Precision.HIGHEST)
    widened = jnp.einsum("xbip,qp->xbiq", narrow, phi_interp, precision=lax.Precision.HIGHEST)
    widened = widened.reshape(2, widened.shape[1] // 8, 8, widened.shape[2], widened.shape[3])
    cosine = jnp.cos(shift_phase)[None]
    sine = jnp.sin(shift_phase)[None]
    real_part = jnp.sum(cosine * widened[0] - sine * widened[1], axis=1)
    imag_part = jnp.sum(cosine * widened[1] + sine * widened[0], axis=1)
    return jnp.stack([real_part, imag_part])


def reference(fine_pattern, fine_partner, fine_offset, fine_count, coarse_partner, coarse_offset, coarse_count, fine_table, coarse_table, theta_start, theta_weight, phi_interp, shift_phase):
    fine_incoming = translate(fine_pattern, fine_table, fine_partner, fine_offset, fine_count)
    coarse_pattern = aggregate(fine_pattern, theta_start, theta_weight, phi_interp, shift_phase)
    coarse_incoming = translate(coarse_pattern, coarse_table, coarse_partner, coarse_offset, coarse_count)
    return fine_incoming, coarse_incoming
```

```python
import functools

import jax
import jax.numpy as jnp
from jax import lax
from jax.experimental import pallas as pl
from jax.experimental.pallas import tpu as pltpu
from jax.sharding import PartitionSpec as P

VMEM = pltpu.VMEM
SMEM = pltpu.SMEM
PARAMS = pltpu.CompilerParams(vmem_limit_bytes=16 * 1024 * 1024)


def spec(space):
    return pl.BlockSpec(memory_space=space)


def swap_cores(x):
    n = lax.axis_size("box")
    return lax.ppermute(x, "box", [(i, i ^ 1) for i in range(n)])


def swap_chips(x):
    n = lax.axis_size("box")
    pairs = [(i, i + 1) for i in range(1, n - 1, 2)]
    return lax.ppermute(x, "box", pairs + [(j, i) for i, j in pairs])


def from_chips(x, distance):
    n = lax.axis_size("box")
    pairs = []
    for i in range(n):
        j = i - 2 * distance if i % 2 == 0 else i + 2 * distance
        if 0 <= j < n:
            pairs.append((j, i))
    return lax.ppermute(x, "box", pairs)


def rim_kernel(pattern_ref, first_ref, last_ref):
    for x in range(2):
        for row in range(2):
            first_ref[x, row] = pattern_ref[x, pl.ds(row, 24, stride=8), :]
            last_ref[x, row] = pattern_ref[x, pl.ds(6 + row, 24, stride=8), :]


def rims(pattern):
    shape = jax.ShapeDtypeStruct((2, 2, 24, 128), jnp.float32)
    return pl.pallas_call(
        rim_kernel,
        out_shape=(shape, shape),
        in_specs=[spec(VMEM)],
        out_specs=(spec(VMEM), spec(VMEM)),
        compiler_params=PARAMS,
    )(pattern.reshape(2, 192, 128))


def aggregate_kernel(pattern_ref, before_ref, after_ref, start_ref, weight_ref, phi_ref, cos_ref, sin_ref, out_ref):
    start = jnp.concatenate([start_ref[...]] * 8, axis=0)
    weight = jnp.concatenate([weight_ref[...]] * 8, axis=0)
    line = lax.broadcasted_iota(jnp.int32, (128, 96), 0)
    column = lax.broadcasted_iota(jnp.int32, (128, 96), 1)
    own = column < 64
    rim = (column - 64) // 8
    row = jnp.where(own, column % 8, jnp.where(rim < 2, rim - 2, rim + 6))
    child = jnp.where(own, column // 8, column % 8)
    row = jnp.where(child == line // 16, row, -100)
    theta = jnp.zeros((128, 96), jnp.float32)
    for q in range(4):
        theta = theta + jnp.where(start + q == row, weight[:, q : q + 1], 0.0)
    phi = phi_ref[...]
    for k in range(3):
        wide = []
        for x in range(2):
            parts = [pattern_ref[x, 64 * k : 64 * k + 64]]
            for rim_ref in (before_ref, after_ref):
                parts += [rim_ref[x, r, 8 * k : 8 * k + 8] for r in range(2)]
            source = jnp.concatenate(parts, axis=0)
            narrow = jnp.dot(
                theta, source, precision=lax.Precision.HIGHEST, preferred_element_type=jnp.float32
            )
            wide.append(
                lax.dot_general(
                    narrow,
                    phi,
                    (((1,), (1,)), ((), ())),
                    precision=lax.Precision.HIGHEST,
                    preferred_element_type=jnp.float32,
                )
            )
        cosine, sine = cos_ref[...], sin_ref[...]
        real_part = (cosine * wide[0] - sine * wide[1]).reshape(8, 16, 256)
        imag_part = (cosine * wide[1] + sine * wide[0]).reshape(8, 16, 256)
        out_ref[0, k] = jnp.sum(real_part, axis=0)
        out_ref[1, k] = jnp.sum(imag_part, axis=0)


def aggregate(pattern, before, after, start, weight, phi, phase):
    phase = phase.reshape(128, 256)
    return pl.pallas_call(
        aggregate_kernel,
        out_shape=jax.ShapeDtypeStruct((2, 3, 16, 256), jnp.float32),
        in_specs=[spec(VMEM)] * 8,
        out_specs=spec(VMEM),
        compiler_params=PARAMS,
    )(pattern.reshape(2, 192, 128), before, after, start, weight, phi, jnp.cos(phase), jnp.sin(phase))


def pairs_sum(window, table, partner_ref, offset_ref, count, b, base):
    sums = None
    for j in range(16):
        place = partner_ref[b, j] - base
        which = jnp.where(j < count, offset_ref[b, j], 16)
        a, c = table[0, which], table[1, which]
        f, g = window[0, place], window[1, place]
        terms = (a * f, c * g, a * g, c * f)
        sums = terms if sums is None else tuple(s + t for s, t in zip(sums, terms))
    return sums[0] - sums[1], sums[2] + sums[3]


def fine_kernel(partner_ref, offset_ref, count_ref, own, inner, outer, table, out_ref, window, operators, sems):
    me = lax.axis_index("box")
    odd = lax.rem(me, 2)
    copies = [
        pltpu.make_async_copy(own, window.at[:, pl.ds(24, 24)], sems.at[0]),
        pltpu.make_async_copy(inner, window.at[:, pl.ds(48 * (1 - odd), 24)], sems.at[1]),
        pltpu.make_async_copy(outer, window.at[:, pl.ds(48 * odd, 24)], sems.at[2]),
        pltpu.make_async_copy(table, operators.at[:, pl.ds(0, 16)], sems.at[3]),
    ]
    for copy in copies:
        copy.start()
    operators[:, 16] = jnp.zeros((2, 8, 128), jnp.float32)
    for copy in copies:
        copy.wait()
    base = (me - 1) * 24

    def step(b, carry):
        real_part, imag_part = pairs_sum(window, operators, partner_ref, offset_ref, count_ref[b], b, base)
        out_ref[0, b] = real_part
        out_ref[1, b] = imag_part
        return carry

    lax.fori_loop(0, 24, step, 0)


def fine_translate(pattern, inner, outer, table, partner, offset, count):
    return pl.pallas_call(
        fine_kernel,
        out_shape=jax.ShapeDtypeStruct((2, 24, 8, 128), jnp.float32),
        in_specs=[spec(SMEM)] * 3 + [spec(pl.ANY)] * 4,
        out_specs=spec(VMEM),
        scratch_shapes=[
            pltpu.VMEM((2, 72, 8, 128), jnp.float32),
            pltpu.VMEM((2, 17, 8, 128), jnp.float32),
            pltpu.SemaphoreType.DMA((4,)),
        ],
        compiler_params=PARAMS,
        cost_estimate=pl.CostEstimate(flops=4_000_000, bytes_accessed=4_000_000, transcendentals=0),
    )(partner, offset, count, pattern, inner, outer, table)


def coarse_kernel(partner_ref, offset_ref, count_ref, pair, near, other, table, out_ref, window, operators, sems):
    me = lax.axis_index("box")
    odd = lax.rem(me, 2)

    def slot(block):
        return window.at[:, pl.ds(3 * block, 3)]

    def part(ref, block):
        return ref.at[:, pl.ds(3 * block, 3)]

    copies = [
        pltpu.make_async_copy(part(pair, 0), slot(4 + odd), sems.at[0]),
        pltpu.make_async_copy(part(pair, 1), slot(5 - odd), sems.at[1]),
        pltpu.make_async_copy(table, operators.at[:, pl.ds(0, 16)], sems.at[2]),
    ]
    for p in range(4):
        copies.append(pltpu.make_async_copy(part(near, p), slot(p + odd * (9 - 2 * p)), sems.at[3 + p]))
        copies.append(pltpu.make_async_copy(part(other, p), slot(9 - p - odd * (9 - 2 * p)), sems.at[7 + p]))
    for copy in copies:
        copy.start()
    operators[:, 16] = jnp.zeros((2, 16, 256), jnp.float32)
    for copy in copies:
        copy.wait()
    base = (me // 2 - 2) * 6

    def step(b, carry):
        real_part, imag_part = pairs_sum(window, operators, partner_ref, offset_ref, count_ref[b], b, base)
        out_ref[0, b] = real_part
        out_ref[1, b] = imag_part
        return carry

    lax.fori_loop(0, 3, step, 0)


def coarse_translate(pair, near, other, table, partner, offset, count):
    return pl.pallas_call(
        coarse_kernel,
        out_shape=jax.ShapeDtypeStruct((2, 3, 16, 256), jnp.float32),
        in_specs=[spec(SMEM)] * 3 + [spec(pl.ANY)] * 4,
        out_specs=spec(VMEM),
        scratch_shapes=[
            pltpu.VMEM((2, 30, 16, 256), jnp.float32),
            pltpu.VMEM((2, 17, 16, 256), jnp.float32),
            pltpu.SemaphoreType.DMA((11,)),
        ],
        compiler_params=PARAMS,
    )(partner, offset, count, pair, near, other, table)


def shards(
    fine_pattern,
    fine_partner,
    fine_offset,
    fine_count,
    coarse_partner,
    coarse_offset,
    coarse_count,
    fine_table,
    coarse_table,
    theta_start,
    theta_weight,
    phi_interp,
    shift_phase,
):
    samp = lax.axis_size("samp")
    first, last = rims(fine_pattern)
    up = [(i, i + 1) for i in range(samp - 1)]
    before = lax.ppermute(last, "samp", up)
    after = lax.ppermute(first, "samp", [(j, i) for i, j in up])
    outer = swap_chips(fine_pattern)
    inner = swap_cores(fine_pattern)
    start = (theta_start - lax.axis_index("samp") * 8)[:, None]
    coarse = aggregate(fine_pattern, before, after, start, theta_weight, phi_interp, shift_phase)
    pair = jnp.concatenate([coarse, swap_cores(coarse)], axis=1)
    near = jnp.concatenate([from_chips(pair, 2), from_chips(pair, 1)], axis=1)
    other = swap_cores(near)
    fine_incoming = fine_translate(
        fine_pattern, inner, outer, fine_table, fine_partner, fine_offset, fine_count
    )
    coarse_incoming = coarse_translate(
        pair, near, other, coarse_table, coarse_partner, coarse_offset, coarse_count
    )
    return (fine_incoming, coarse_incoming)


def solution(mesh):
    return jax.shard_map(
        shards,
        mesh=mesh,
        in_specs=(
            P(None, "box", "samp", None),
            P("box", None),
            P("box", None),
            P("box"),
            P("box", None),
            P("box", None),
            P("box"),
            P(None, None, "samp", None),
            P(None, None, "samp", None),
            P("samp"),
            P("samp", None),
            P(),
            P(None, "samp", None),
        ),
        out_specs=(P(None, "box", "samp", None), P(None, "box", "samp", None)),
        check_vma=False,
    )
```

```python
import functools

import jax
import jax.numpy as jnp
from jax import lax
from jax.experimental import pallas as pl
from jax.experimental.pallas import tpu as pltpu
from jax.sharding import PartitionSpec as P

VMEM = pltpu.VMEM
SMEM = pltpu.SMEM
PARAMS = pltpu.CompilerParams(vmem_limit_bytes=16 * 1024 * 1024)


def spec(space):
    return pl.BlockSpec(memory_space=space)


def matched(x, axis, pairs):
    return lax.ppermute(x, axis, pairs + [(j, i) for i, j in pairs])


def swap_cores(x):
    n = lax.axis_size("box")
    return matched(x, "box", [(i, i + 1) for i in range(0, n, 2)])


def swap_chips(x, core, distance):
    n = lax.axis_size("box")
    pairs = [(i + core, i + 2 * distance + 1 - core) for i in range(0, n - 2 * distance, 2)]
    return matched(x, "box", pairs)


def swap_rims(x, start):
    n = lax.axis_size("samp")
    return matched(x, "samp", [(i, i + 1) for i in range(start, n - 1, 2)])


def rim_kernel(pattern_ref, even_ref, odd_ref):
    odd = lax.rem(lax.axis_index("samp"), 2) == 1
    for x in range(2):
        for row in range(2):
            first = pattern_ref[x, pl.ds(row, 24, stride=8), :]
            last = pattern_ref[x, pl.ds(6 + row, 24, stride=8), :]
            even_ref[x, row] = jnp.where(odd, first, last)
            odd_ref[x, row] = jnp.where(odd, last, first)


def rims(pattern):
    shape = jax.ShapeDtypeStruct((2, 2, 24, 128), jnp.float32)
    return pl.pallas_call(
        rim_kernel,
        out_shape=(shape, shape),
        in_specs=[spec(VMEM)],
        out_specs=(spec(VMEM), spec(VMEM)),
        compiler_params=PARAMS,
    )(pattern)


def aggregate_kernel(pattern_ref, even_ref, odd_ref, start_ref, weight_ref, phi_ref, cos_ref, sin_ref, out_ref, both_ref):
    start = jnp.concatenate([start_ref[...]] * 8, axis=0)
    weight = jnp.concatenate([weight_ref[...]] * 8, axis=0)
    line = lax.broadcasted_iota(jnp.int32, (128, 96), 0)
    column = lax.broadcasted_iota(jnp.int32, (128, 96), 1)
    own = column < 64
    rim = (column - 64) // 8
    odd = lax.rem(lax.axis_index("samp"), 2) == 1
    rim = jnp.where((rim < 2) == odd, rim % 2 - 2, rim % 2 + 8)
    row = jnp.where(own, column % 8, rim)
    child = jnp.where(own, column // 8, column % 8)
    row = jnp.where(child == line // 16, row, -100)
    theta = jnp.zeros((128, 96), jnp.float32)
    for q in range(4):
        theta = theta + jnp.where(start + q == row, weight[:, q : q + 1], 0.0)
    phi = phi_ref[...]
    both_ref[:, 96:] = pattern_ref[...]
    for k in range(3):
        wide = []
        for x in range(2):
            parts = [pattern_ref[x, 64 * k : 64 * k + 64]]
            for rim_ref in (even_ref, odd_ref):
                parts += [rim_ref[x, r, 8 * k : 8 * k + 8] for r in range(2)]
            source = jnp.concatenate(parts, axis=0)
            narrow = jnp.dot(
                theta, source, precision=lax.Precision.HIGHEST, preferred_element_type=jnp.float32
            )
            wide.append(
                lax.dot_general(
                    narrow,
                    phi,
                    (((1,), (1,)), ((), ())),
                    precision=lax.Precision.HIGHEST,
                    preferred_element_type=jnp.float32,
                )
            )
        cosine, sine = cos_ref[...], sin_ref[...]
        real_part = (cosine * wide[0] - sine * wide[1]).reshape(8, 16, 256)
        imag_part = (cosine * wide[1] + sine * wide[0]).reshape(8, 16, 256)
        for x, value in enumerate((real_part, imag_part)):
            value = jnp.sum(value, axis=0)
            for half in range(2):
                rows = pl.ds(32 * k + 16 * half, 16)
                out_ref[x, rows] = value[:, 128 * half : 128 * half + 128]
                both_ref[x, rows] = value[:, 128 * half : 128 * half + 128]


def aggregate(pattern, even, odd, start, weight, phi, phase):
    phase = phase.reshape(128, 256)
    return pl.pallas_call(
        aggregate_kernel,
        out_shape=(
            jax.ShapeDtypeStruct((2, 96, 128), jnp.float32),
            jax.ShapeDtypeStruct((2, 288, 128), jnp.float32),
        ),
        in_specs=[spec(VMEM)] * 8,
        out_specs=(spec(VMEM), spec(VMEM)),
        compiler_params=PARAMS,
    )(pattern, even, odd, start, weight, phi, jnp.cos(phase), jnp.sin(phase))


def pairs_sum(window, table, lines, partner_ref, offset_ref, count, b, base):
    sums = None
    for j in range(16):
        place = pl.multiple_of((partner_ref[b, j] - base) * lines, lines)
        which = pl.multiple_of(jnp.where(j < count, offset_ref[b, j], 16) * lines, lines)
        a, c = table[0, pl.ds(which, lines)], table[1, pl.ds(which, lines)]
        f, g = window[0, pl.ds(place, lines)], window[1, pl.ds(place, lines)]
        terms = (a * f, c * g, a * g, c * f)
        sums = terms if sums is None else tuple(s + t for s, t in zip(sums, terms))
    return sums[0] - sums[1], sums[2] + sums[3]


def fine_kernel(partner_ref, offset_ref, count_ref, own, inner, outer, table, out_ref, window, operators, sems):
    me = lax.axis_index("box")
    odd = lax.rem(me, 2)
    copies = [
        pltpu.make_async_copy(own, window.at[:, pl.ds(192, 192)], sems.at[0]),
        pltpu.make_async_copy(inner, window.at[:, pl.ds(384 * (1 - odd), 192)], sems.at[1]),
        pltpu.make_async_copy(outer.at[:, pl.ds(96, 192)], window.at[:, pl.ds(384 * odd, 192)], sems.at[2]),
        pltpu.make_async_copy(table, operators.at[:, pl.ds(0, 128)], sems.at[3]),
    ]
    for copy in copies:
        copy.start()
    operators[:, 128:] = jnp.zeros((2, 8, 128), jnp.float32)
    for copy in copies:
        copy.wait()
    base = (me - 1) * 24

    def step(b, carry):
        real_part, imag_part = pairs_sum(window, operators, 8, partner_ref, offset_ref, count_ref[b], b, base)
        out_ref[0, b] = real_part
        out_ref[1, b] = imag_part
        return carry

    lax.fori_loop(0, 24, step, 0)


def fine_translate(pattern, inner, outer, table, partner, offset, count):
    return pl.pallas_call(
        fine_kernel,
        out_shape=jax.ShapeDtypeStruct((2, 24, 8, 128), jnp.float32),
        in_specs=[spec(SMEM)] * 3 + [spec(pl.ANY)] * 4,
        out_specs=spec(VMEM),
        scratch_shapes=[
            pltpu.VMEM((2, 576, 128), jnp.float32),
            pltpu.VMEM((2, 136, 128), jnp.float32),
            pltpu.SemaphoreType.DMA((4,)),
        ],
        compiler_params=PARAMS,
        cost_estimate=pl.CostEstimate(flops=4_000_000, bytes_accessed=4_000_000, transcendentals=0),
    )(partner, offset, count, pattern, inner, outer, table.reshape(2, 128, 128))


def coarse_kernel(partner_ref, offset_ref, count_ref, mine, theirs, table, out_ref, window, operators, sems):
    me = lax.axis_index("box")
    odd = lax.rem(me, 2)
    copies = []
    for source, core, first in ((mine, odd, 0), (theirs, 1 - odd, 5)):
        slots = (4 + core, 3 + 3 * core, 7 - 5 * core, 1 + 7 * core, 9 - 9 * core)
        for p, slot in enumerate(slots):
            copies.append(
                pltpu.make_async_copy(
                    source.at[:, pl.ds(96 * p, 96)],
                    window.at[:, pl.ds(pl.multiple_of(96 * slot, 96), 96)],
                    sems.at[first + p],
                )
            )
    for half in range(2):
        copies.append(
            pltpu.make_async_copy(
                table.at[:, :, :, pl.ds(128 * half, 128)],
                operators.at[:, pl.ds(0, 16), pl.ds(16 * half, 16)],
                sems.at[10 + half],
            )
        )
    for copy in copies:
        copy.start()
    operators[:, 16] = jnp.zeros((2, 32, 128), jnp.float32)
    for copy in copies:
        copy.wait()
    base = (me // 2 - 2) * 6
    flat = operators.reshape(2, 17 * 32, 128)

    def step(b, carry):
        parts = pairs_sum(window, flat, 32, partner_ref, offset_ref, count_ref[b], b, base)
        for x in range(2):
            for half in range(2):
                out_ref[x, b, :, 128 * half : 128 * half + 128] = parts[x][16 * half : 16 * half + 16]
        return carry

    lax.fori_loop(0, 3, step, 0)


def coarse_translate(mine, theirs, table, partner, offset, count):
    return pl.pallas_call(
        coarse_kernel,
        out_shape=jax.ShapeDtypeStruct((2, 3, 16, 256), jnp.float32),
        in_specs=[spec(SMEM)] * 3 + [spec(pl.ANY)] * 3,
        out_specs=spec(VMEM),
        scratch_shapes=[
            pltpu.VMEM((2, 960, 128), jnp.float32),
            pltpu.VMEM((2, 17, 32, 128), jnp.float32),
            pltpu.SemaphoreType.DMA((12,)),
        ],
        compiler_params=PARAMS,
    )(partner, offset, count, mine, theirs, table)


def shards(
    fine_pattern,
    fine_partner,
    fine_offset,
    fine_count,
    coarse_partner,
    coarse_offset,
    coarse_count,
    fine_table,
    coarse_table,
    theta_start,
    theta_weight,
    phi_interp,
    shift_phase,
):
    pattern = fine_pattern.reshape(2, 192, 128)
    even, odd = rims(pattern)
    even, odd, pattern = lax.optimization_barrier((even, odd, pattern))
    even, odd = swap_rims(even, 0), swap_rims(odd, 1)
    inner = swap_cores(pattern)
    even, odd, inner = lax.optimization_barrier((even, odd, inner))
    start = (theta_start - lax.axis_index("samp") * 8)[:, None]
    coarse, both = aggregate(pattern, even, odd, start, theta_weight, phi_interp, shift_phase)
    outer = swap_chips(both, 1, 1)
    others = [swap_chips(coarse, 0, 1), swap_chips(coarse, 1, 2), swap_chips(coarse, 0, 2)]
    mine = jnp.concatenate([coarse, outer[:, :96]] + others, axis=1)
    theirs = swap_cores(mine)
    fine_incoming = fine_translate(
        pattern, inner, outer, fine_table, fine_partner, fine_offset, fine_count
    )
    coarse_incoming = coarse_translate(
        mine, theirs, coarse_table, coarse_partner, coarse_offset, coarse_count
    )
    return (fine_incoming, coarse_incoming)


def solution(mesh):
    return jax.shard_map(
        shards,
        mesh=mesh,
        in_specs=(
            P(None, "box", "samp", None),
            P("box", None),
            P("box", None),
            P("box"),
            P("box", None),
            P("box", None),
            P("box"),
            P(None, None, "samp", None),
            P(None, None, "samp", None),
            P("samp"),
            P("samp", None),
            P(),
            P(None, "samp", None),
        ),
        out_specs=(P(None, "box", "samp", None), P(None, "box", "samp", None)),
        check_vma=False,
    )
```

```python
import functools

import jax
import jax.numpy as jnp
from jax import lax
from jax.experimental import pallas as pl
from jax.experimental.pallas import tpu as pltpu
from jax.sharding import PartitionSpec as P

VMEM = pltpu.VMEM
SMEM = pltpu.SMEM
PARAMS = pltpu.CompilerParams(vmem_limit_bytes=16 * 1024 * 1024)


def spec(space):
    return pl.BlockSpec(memory_space=space)


def matched(x, axis, pairs):
    return lax.ppermute(x, axis, pairs + [(j, i) for i, j in pairs])


def swap_cores(x):
    n = lax.axis_size("box")
    return matched(x, "box", [(i, i + 1) for i in range(0, n, 2)])


def swap_chips(x, core, distance):
    n = lax.axis_size("box")
    pairs = [(i + core, i + 2 * distance + 1 - core) for i in range(0, n - 2 * distance, 2)]
    return matched(x, "box", pairs)


def swap_rims(x, start):
    n = lax.axis_size("samp")
    return matched(x, "samp", [(i, i + 1) for i in range(start, n - 1, 2)])


def rim_kernel(own_ref, inner_ref, even_ref, odd_ref):
    odd = lax.rem(lax.axis_index("samp"), 2) == 1
    for x in range(2):
        for row in range(2):
            for which, ref in enumerate((own_ref, inner_ref)):
                first = ref[x, pl.ds(row, 24, stride=8), :]
                last = ref[x, pl.ds(6 + row, 24, stride=8), :]
                boxes = pl.ds(24 * which, 24)
                even_ref[x, row, boxes] = jnp.where(odd, first, last)
                odd_ref[x, row, boxes] = jnp.where(odd, last, first)


def rims(own, inner):
    shape = jax.ShapeDtypeStruct((2, 2, 48, 128), jnp.float32)
    return pl.pallas_call(
        rim_kernel,
        out_shape=(shape, shape),
        in_specs=[spec(VMEM)] * 2,
        out_specs=(spec(VMEM), spec(VMEM)),
        compiler_params=PARAMS,
    )(own, inner)


def split(x):
    high = x.astype(jnp.bfloat16)
    return high, (x - high.astype(jnp.float32)).astype(jnp.bfloat16)


def dot(x, y):
    return jnp.dot(x, y, preferred_element_type=jnp.float32)


def matrices_kernel(start_ref, weight_ref, phi_ref, theta_ref, theta_low_ref, phi_out_ref, phi_low_ref):
    start = jnp.concatenate([start_ref[...]] * 8, axis=0)
    weight = jnp.concatenate([weight_ref[...]] * 8, axis=0)
    line = lax.broadcasted_iota(jnp.int32, (128, 96), 0)
    column = lax.broadcasted_iota(jnp.int32, (128, 96), 1)
    own = column < 64
    rim = (column - 64) // 8
    odd = lax.rem(lax.axis_index("samp"), 2) == 1
    rim = jnp.where((rim < 2) == odd, rim % 2 - 2, rim % 2 + 8)
    row = jnp.where(own, column % 8, rim)
    child = jnp.where(own, column // 8, column % 8)
    row = jnp.where(child == line // 16, row, -100)
    theta = jnp.zeros((128, 96), jnp.float32)
    for q in range(4):
        theta = theta + jnp.where(start + q == row, weight[:, q : q + 1], 0.0)
    high, low = split(theta)
    theta_ref[...] = jnp.concatenate([high, high], axis=1)
    theta_low_ref[...] = low
    high, low = split(phi_ref[...].T)
    phi_out_ref[...] = jnp.concatenate([high, high], axis=0)
    phi_low_ref[...] = low


def matrices(start, weight, phi):
    shapes = ((128, 192), (128, 96), (256, 256), (128, 256))
    return pl.pallas_call(
        matrices_kernel,
        out_shape=tuple(jax.ShapeDtypeStruct(s, jnp.bfloat16) for s in shapes),
        in_specs=[spec(VMEM)] * 3,
        out_specs=(spec(VMEM),) * 4,
        compiler_params=PARAMS,
    )(start, weight, phi)


def aggregate_kernel(
    own_ref, inner_ref, even_ref, odd_ref, theta_ref, theta_low_ref, phi_ref, phi_low_ref, cos_ref, sin_ref, pair_ref, both_ref
):
    me = lax.rem(lax.axis_index("box"), 2)
    theta, theta_low = theta_ref[...], theta_low_ref[...]
    phi, phi_low = phi_ref[...], phi_low_ref[...]
    both_ref[:, 192:] = own_ref[...]
    for which, ref in enumerate((own_ref, inner_ref)):
        place = 96 * (me if which == 0 else 1 - me)
        for k in range(3):
            columns = []
            for x in range(2):
                parts = [ref[x, 64 * k : 64 * k + 64]]
                for rim_ref in (even_ref, odd_ref):
                    parts += [rim_ref[x, r, pl.ds(24 * which + 8 * k, 8)] for r in range(2)]
                columns.append(jnp.concatenate(parts, axis=0))
            high, low = split(jnp.concatenate(columns, axis=1))
            narrow = dot(theta, jnp.concatenate([high, low], axis=0)) + dot(theta_low, high)
            high, low = split(narrow)
            wide = []
            for x in range(2):
                part = slice(128 * x, 128 * x + 128)
                both = jnp.concatenate([high[:, part], low[:, part]], axis=1)
                wide.append(dot(both, phi) + dot(high[:, part], phi_low))
            cosine, sine = cos_ref[...], sin_ref[...]
            real_part = (cosine * wide[0] - sine * wide[1]).reshape(8, 16, 256)
            imag_part = (cosine * wide[1] + sine * wide[0]).reshape(8, 16, 256)
            for x, value in enumerate((real_part, imag_part)):
                value = jnp.sum(value, axis=0)
                for half in range(2):
                    rows = pl.ds(pl.multiple_of(place + 32 * k + 16 * half, 16), 16)
                    pair_ref[x, rows] = value[:, 128 * half : 128 * half + 128]
                    both_ref[x, rows] = value[:, 128 * half : 128 * half + 128]


def aggregate(own, inner, even, odd, mats, cosine, sine):
    return pl.pallas_call(
        aggregate_kernel,
        out_shape=(
            jax.ShapeDtypeStruct((2, 192, 128), jnp.float32),
            jax.ShapeDtypeStruct((2, 384, 128), jnp.float32),
        ),
        in_specs=[spec(VMEM)] * 10,
        out_specs=(spec(VMEM), spec(VMEM)),
        compiler_params=PARAMS,
    )(own, inner, even, odd, *mats, cosine, sine)


def fine_kernel(partner_ref, offset_ref, count_ref, own, inner, outer, table, out_ref, window, operators, sems):
    me = lax.axis_index("box")
    odd = lax.rem(me, 2)
    copies = [
        pltpu.make_async_copy(own, window.at[:, pl.ds(192, 192)], sems.at[0]),
        pltpu.make_async_copy(inner, window.at[:, pl.ds(384 * (1 - odd), 192)], sems.at[1]),
        pltpu.make_async_copy(outer.at[:, pl.ds(192, 192)], window.at[:, pl.ds(384 * odd, 192)], sems.at[2]),
        pltpu.make_async_copy(table, operators.at[:, pl.ds(0, 128)], sems.at[3]),
    ]
    for copy in copies:
        copy.start()
    operators[:, 128:] = jnp.zeros((2, 8, 128), jnp.float32)
    for copy in copies:
        copy.wait()
    base = (me - 1) * 24

    def step(b, carry):
        sums = None
        for j in range(16):
            place = pl.multiple_of((partner_ref[b, j] - base) * 8, 8)
            which = pl.multiple_of(jnp.where(j < count_ref[b], offset_ref[b, j], 16) * 8, 8)
            a, c = operators[0, pl.ds(which, 8)], operators[1, pl.ds(which, 8)]
            f, g = window[0, pl.ds(place, 8)], window[1, pl.ds(place, 8)]
            terms = (a * f, c * g, a * g, c * f)
            sums = terms if sums is None else tuple(s + t for s, t in zip(sums, terms))
        out_ref[0, b] = sums[0] - sums[1]
        out_ref[1, b] = sums[2] + sums[3]
        return carry

    lax.fori_loop(0, 24, step, 0)


def fine_translate(pattern, inner, outer, table, partner, offset, count):
    return pl.pallas_call(
        fine_kernel,
        out_shape=jax.ShapeDtypeStruct((2, 24, 8, 128), jnp.float32),
        in_specs=[spec(SMEM)] * 3 + [spec(pl.ANY)] * 4,
        out_specs=spec(VMEM),
        scratch_shapes=[
            pltpu.VMEM((2, 576, 128), jnp.float32),
            pltpu.VMEM((2, 136, 128), jnp.float32),
            pltpu.SemaphoreType.DMA((4,)),
        ],
        compiler_params=PARAMS,
        cost_estimate=pl.CostEstimate(flops=4_000_000, bytes_accessed=40_000_000, transcendentals=0),
    )(partner, offset, count, pattern, inner, outer, table.reshape(2, 128, 128))


def coarse_sums(window, table, partner_ref, offset_ref, count_ref, b, near):
    me = lax.axis_index("box")
    odd = lax.rem(me, 2) == 1
    base = (me // 2 - 2) * 6
    sums = [None, None]
    for j in range(16):
        place = partner_ref[b, j] - base
        side = jnp.where(odd, place >= 12, place < 18)
        live = jnp.logical_and(j < count_ref[b], side if near else jnp.logical_not(side))
        place = jnp.where(place >= 24, place - 24, jnp.where(place >= 18, place - 12, place))
        place = pl.multiple_of(jnp.where(live, place, 0) * 32, 32)
        scale = jnp.where(live, 1.0, 0.0)
        which = offset_ref[b, j]
        for half in range(2):
            lanes = slice(128 * half, 128 * half + 128)
            a, c = table[0, which, :, lanes] * scale, table[1, which, :, lanes] * scale
            f, g = window[0, pl.ds(place + 16 * half, 16)], window[1, pl.ds(place + 16 * half, 16)]
            terms = (a * f, c * g, a * g, c * f)
            old = sums[half]
            sums[half] = terms if old is None else tuple(s + t for s, t in zip(old, terms))
    return [(s[0] - s[1], s[2] + s[3]) for s in sums]


def near_kernel(partner_ref, offset_ref, count_ref, pair, sides, table, out_ref, window, sems):
    copies = [
        pltpu.make_async_copy(sides, window.at[:, pl.ds(0, 384)], sems.at[0]),
        pltpu.make_async_copy(pair, window.at[:, pl.ds(384, 192)], sems.at[1]),
    ]
    for copy in copies:
        copy.start()
    for copy in copies:
        copy.wait()

    def step(b, carry):
        sums = coarse_sums(window, table, partner_ref, offset_ref, count_ref, b, True)
        for half in range(2):
            for x in range(2):
                out_ref[x, b, :, 128 * half : 128 * half + 128] = sums[half][x]
        return carry

    lax.fori_loop(0, 3, step, 0)


def far_kernel(partner_ref, offset_ref, count_ref, other, table, part_ref, out_ref):
    def step(b, carry):
        sums = coarse_sums(other, table, partner_ref, offset_ref, count_ref, b, False)
        for half in range(2):
            lanes = slice(128 * half, 128 * half + 128)
            for x in range(2):
                out_ref[x, b, :, lanes] = part_ref[x, b, :, lanes] + sums[half][x]
        return carry

    lax.fori_loop(0, 3, step, 0)


def near_translate(pair, sides, table, partner, offset, count):
    return pl.pallas_call(
        near_kernel,
        out_shape=jax.ShapeDtypeStruct((2, 3, 16, 256), jnp.float32),
        in_specs=[spec(SMEM)] * 3 + [spec(pl.ANY)] * 2 + [spec(VMEM)],
        out_specs=spec(VMEM),
        scratch_shapes=[pltpu.VMEM((2, 576, 128), jnp.float32), pltpu.SemaphoreType.DMA((2,))],
        compiler_params=PARAMS,
    )(partner, offset, count, pair, sides, table)


def far_translate(other, table, part, partner, offset, count):
    return pl.pallas_call(
        far_kernel,
        out_shape=jax.ShapeDtypeStruct((2, 3, 16, 256), jnp.float32),
        in_specs=[spec(SMEM)] * 3 + [spec(VMEM)] * 3,
        out_specs=spec(VMEM),
        compiler_params=PARAMS,
    )(partner, offset, count, other, table, part)


def shards(
    fine_pattern,
    fine_partner,
    fine_offset,
    fine_count,
    coarse_partner,
    coarse_offset,
    coarse_count,
    fine_table,
    coarse_table,
    theta_start,
    theta_weight,
    phi_interp,
    shift_phase,
):
    pattern = fine_pattern.reshape(2, 192, 128)
    inner = swap_cores(pattern)
    start = (theta_start - lax.axis_index("samp") * 8)[:, None]
    mats = matrices(start, theta_weight, phi_interp)
    phase = shift_phase.reshape(128, 256)
    waves = (jnp.cos(phase), jnp.sin(phase))
    inner, mats, waves = lax.optimization_barrier((inner, mats, waves))
    even, odd = rims(pattern, inner)
    even, odd = swap_rims(even, 0), swap_rims(odd, 1)
    pair, both = aggregate(pattern, inner, even, odd, mats, *waves)
    outer = swap_chips(both, 1, 1)
    distant = swap_chips(pair, 1, 2)
    fine_incoming = fine_translate(
        pattern, inner, outer, fine_table, fine_partner, fine_offset, fine_count
    )
    distant, fine_incoming = lax.optimization_barrier((distant, fine_incoming))
    sides = jnp.concatenate([distant, outer[:, :192]], axis=1)
    other = swap_cores(sides)
    part = near_translate(pair, sides, coarse_table, coarse_partner, coarse_offset, coarse_count)
    coarse_incoming = far_translate(
        other, coarse_table, part, coarse_partner, coarse_offset, coarse_count
    )
    return (fine_incoming, coarse_incoming)


def solution(mesh):
    return jax.shard_map(
        shards,
        mesh=mesh,
        in_specs=(
            P(None, "box", "samp", None),
            P("box", None),
            P("box", None),
            P("box"),
            P("box", None),
            P("box", None),
            P("box"),
            P(None, None, "samp", None),
            P(None, None, "samp", None),
            P("samp"),
            P("samp", None),
            P(),
            P(None, "samp", None),
        ),
        out_specs=(P(None, "box", "samp", None), P(None, "box", "samp", None)),
        check_vma=False,
    )
```

```python
import functools

import jax
import jax.numpy as jnp
from jax import lax
from jax.experimental import pallas as pl
from jax.experimental.pallas import tpu as pltpu
from jax.sharding import PartitionSpec as P

VMEM = pltpu.VMEM
SMEM = pltpu.SMEM
PARAMS = pltpu.CompilerParams(vmem_limit_bytes=16 * 1024 * 1024)


def spec(space):
    return pl.BlockSpec(memory_space=space)


def matched(x, axis, pairs):
    return lax.ppermute(x, axis, pairs + [(j, i) for i, j in pairs])


def swap_cores(x):
    n = lax.axis_size("box")
    return matched(x, "box", [(i, i + 1) for i in range(0, n, 2)])


def swap_chips(x, core, distance):
    n = lax.axis_size("box")
    pairs = [(i + core, i + 2 * distance + 1 - core) for i in range(0, n - 2 * distance, 2)]
    return matched(x, "box", pairs)


def swap_rims(x, start):
    n = lax.axis_size("samp")
    return matched(x, "samp", [(i, i + 1) for i in range(start, n - 1, 2)])


def rim_kernel(own_ref, inner_ref, even_ref, odd_ref):
    odd = lax.rem(lax.axis_index("samp"), 2) == 1
    for x in range(2):
        for row in range(2):
            for which, ref in enumerate((own_ref, inner_ref)):
                first = ref[x, pl.ds(row, 24, stride=8), :]
                last = ref[x, pl.ds(6 + row, 24, stride=8), :]
                boxes = pl.ds(24 * which, 24)
                even_ref[x, row, boxes] = jnp.where(odd, first, last)
                odd_ref[x, row, boxes] = jnp.where(odd, last, first)


def rims(own, inner):
    shape = jax.ShapeDtypeStruct((2, 2, 48, 128), jnp.float32)
    return pl.pallas_call(
        rim_kernel,
        out_shape=(shape, shape),
        in_specs=[spec(VMEM)] * 2,
        out_specs=(spec(VMEM), spec(VMEM)),
        compiler_params=PARAMS,
    )(own, inner)


def split(x):
    high = x.astype(jnp.bfloat16)
    return high, (x - high.astype(jnp.float32)).astype(jnp.bfloat16)


def dot(x, y):
    return jnp.dot(x, y, preferred_element_type=jnp.float32)


def matrices_kernel(start_ref, weight_ref, phi_ref, theta_ref, theta_low_ref, phi_out_ref, phi_low_ref):
    samp = lax.axis_index("samp")
    line = lax.broadcasted_iota(jnp.int32, (16, 96), 0)
    column = lax.broadcasted_iota(jnp.int32, (16, 96), 1)
    rim = (column - 64) // 8
    rim = jnp.where((rim < 2) == (lax.rem(samp, 2) == 1), rim % 2 - 2, rim % 2 + 8)
    row = jnp.where(column < 64, column % 8, rim) + samp * 8
    theta = jnp.zeros((16, 96), jnp.float32)
    for i in range(16):
        for q in range(4):
            theta = theta + jnp.where((row == start_ref[i] + q) & (line == i), weight_ref[q, i], 0.0)
    theta = jnp.concatenate([theta] * 8, axis=0)
    line = lax.broadcasted_iota(jnp.int32, (128, 96), 0)
    column = lax.broadcasted_iota(jnp.int32, (128, 96), 1)
    child = jnp.where(column < 64, column // 8, column % 8)
    theta = jnp.where(child == line // 16, theta, 0.0)
    high, low = split(theta)
    theta_ref[...] = jnp.concatenate([high, high], axis=1)
    theta_low_ref[...] = low
    high, low = split(phi_ref[...].T)
    phi_out_ref[...] = jnp.concatenate([high, high], axis=0)
    phi_low_ref[...] = low


def matrices(start, weight, phi):
    shapes = ((128, 192), (128, 96), (256, 256), (128, 256))
    return pl.pallas_call(
        matrices_kernel,
        out_shape=tuple(jax.ShapeDtypeStruct(s, jnp.bfloat16) for s in shapes),
        in_specs=[spec(SMEM), spec(SMEM), spec(VMEM)],
        out_specs=(spec(VMEM),) * 4,
        compiler_params=PARAMS,
    )(start, weight.T, phi)


def aggregate_kernel(
    own_ref, inner_ref, even_ref, odd_ref, theta_ref, theta_low_ref, phi_ref, phi_low_ref, cos_ref, sin_ref, pair_ref
):
    me = lax.rem(lax.axis_index("box"), 2)
    theta, theta_low = theta_ref[...], theta_low_ref[...]
    phi, phi_low = phi_ref[...], phi_low_ref[...]
    for which, ref in enumerate((own_ref, inner_ref)):
        place = 96 * (me if which == 0 else 1 - me)
        for k in range(3):
            columns = []
            for x in range(2):
                parts = [ref[x, 64 * k : 64 * k + 64]]
                for rim_ref in (even_ref, odd_ref):
                    parts += [rim_ref[x, r, pl.ds(24 * which + 8 * k, 8)] for r in range(2)]
                columns.append(jnp.concatenate(parts, axis=0))
            high, low = split(jnp.concatenate(columns, axis=1))
            narrow = dot(theta, jnp.concatenate([high, low], axis=0)) + dot(theta_low, high)
            high, low = split(narrow)
            wide = []
            for x in range(2):
                part = slice(128 * x, 128 * x + 128)
                both = jnp.concatenate([high[:, part], low[:, part]], axis=1)
                wide.append(dot(both, phi) + dot(high[:, part], phi_low))
            cosine, sine = cos_ref[...], sin_ref[...]
            real_part = (cosine * wide[0] - sine * wide[1]).reshape(8, 16, 256)
            imag_part = (cosine * wide[1] + sine * wide[0]).reshape(8, 16, 256)
            for x, value in enumerate((real_part, imag_part)):
                value = jnp.sum(value, axis=0)
                for half in range(2):
                    rows = pl.ds(pl.multiple_of(place + 32 * k + 16 * half, 16), 16)
                    pair_ref[x, rows] = value[:, 128 * half : 128 * half + 128]


def aggregate(own, inner, even, odd, mats, cosine, sine):
    return pl.pallas_call(
        aggregate_kernel,
        out_shape=jax.ShapeDtypeStruct((2, 192, 128), jnp.float32),
        in_specs=[spec(VMEM)] * 10,
        out_specs=spec(VMEM),
        compiler_params=PARAMS,
    )(own, inner, even, odd, *mats, cosine, sine)


def fine_kernel(partner_ref, offset_ref, count_ref, own, inner, outer, table, out_ref, window, operators, sems):
    me = lax.axis_index("box")
    odd = lax.rem(me, 2)
    copies = [
        pltpu.make_async_copy(own, window.at[:, pl.ds(192, 192)], sems.at[0]),
        pltpu.make_async_copy(inner, window.at[:, pl.ds(384 * (1 - odd), 192)], sems.at[1]),
        pltpu.make_async_copy(outer, window.at[:, pl.ds(384 * odd, 192)], sems.at[2]),
        pltpu.make_async_copy(table, operators.at[:, pl.ds(0, 128)], sems.at[3]),
    ]
    for copy in copies:
        copy.start()
    operators[:, 128:] = jnp.zeros((2, 8, 128), jnp.float32)
    for copy in copies:
        copy.wait()
    base = (me - 1) * 24

    def step(b, carry):
        sums = None
        for j in range(16):
            place = pl.multiple_of((partner_ref[b, j] - base) * 8, 8)
            which = pl.multiple_of(jnp.where(j < count_ref[b], offset_ref[b, j], 16) * 8, 8)
            a, c = operators[0, pl.ds(which, 8)], operators[1, pl.ds(which, 8)]
            f, g = window[0, pl.ds(place, 8)], window[1, pl.ds(place, 8)]
            terms = (a * f, c * g, a * g, c * f)
            sums = terms if sums is None else tuple(s + t for s, t in zip(sums, terms))
        out_ref[0, b] = sums[0] - sums[1]
        out_ref[1, b] = sums[2] + sums[3]
        return carry

    lax.fori_loop(0, 24, step, 0)


def fine_translate(pattern, inner, outer, table, partner, offset, count):
    return pl.pallas_call(
        fine_kernel,
        out_shape=jax.ShapeDtypeStruct((2, 24, 8, 128), jnp.float32),
        in_specs=[spec(SMEM)] * 3 + [spec(pl.ANY)] * 4,
        out_specs=spec(VMEM),
        scratch_shapes=[
            pltpu.VMEM((2, 576, 128), jnp.float32),
            pltpu.VMEM((2, 136, 128), jnp.float32),
            pltpu.SemaphoreType.DMA((4,)),
        ],
        compiler_params=PARAMS,
        cost_estimate=pl.CostEstimate(flops=4_000_000, bytes_accessed=40_000_000, transcendentals=0),
    )(partner, offset, count, pattern, inner, outer, table.reshape(2, 128, 128))


def coarse_sums(window, table, partner_ref, offset_ref, count_ref, b, near):
    me = lax.axis_index("box")
    odd = lax.rem(me, 2) == 1
    base = (me // 2 - 2) * 6
    sums = [None, None]
    for j in range(16):
        place = partner_ref[b, j] - base
        side = jnp.where(odd, place >= 12, place < 18)
        live = jnp.logical_and(j < count_ref[b], side if near else jnp.logical_not(side))
        place = jnp.where(place >= 24, place - 24, jnp.where(place >= 18, place - 12, place))
        place = pl.multiple_of(jnp.where(live, place, 0) * 32, 32)
        scale = jnp.where(live, 1.0, 0.0)
        which = offset_ref[b, j]
        for half in range(2):
            lanes = slice(128 * half, 128 * half + 128)
            a, c = table[0, which, :, lanes] * scale, table[1, which, :, lanes] * scale
            f, g = window[0, pl.ds(place + 16 * half, 16)], window[1, pl.ds(place + 16 * half, 16)]
            terms = (a * f, c * g, a * g, c * f)
            old = sums[half]
            sums[half] = terms if old is None else tuple(s + t for s, t in zip(old, terms))
    return [(s[0] - s[1], s[2] + s[3]) for s in sums]


def near_kernel(partner_ref, offset_ref, count_ref, pair, sides, table, out_ref, window, sems):
    copies = [
        pltpu.make_async_copy(sides, window.at[:, pl.ds(0, 384)], sems.at[0]),
        pltpu.make_async_copy(pair, window.at[:, pl.ds(384, 192)], sems.at[1]),
    ]
    for copy in copies:
        copy.start()
    for copy in copies:
        copy.wait()

    def step(b, carry):
        sums = coarse_sums(window, table, partner_ref, offset_ref, count_ref, b, True)
        for half in range(2):
            for x in range(2):
                out_ref[x, b, :, 128 * half : 128 * half + 128] = sums[half][x]
        return carry

    lax.fori_loop(0, 3, step, 0)


def far_kernel(partner_ref, offset_ref, count_ref, other, table, part_ref, out_ref):
    def step(b, carry):
        sums = coarse_sums(other, table, partner_ref, offset_ref, count_ref, b, False)
        for half in range(2):
            lanes = slice(128 * half, 128 * half + 128)
            for x in range(2):
                out_ref[x, b, :, lanes] = part_ref[x, b, :, lanes] + sums[half][x]
        return carry

    lax.fori_loop(0, 3, step, 0)


def near_translate(pair, sides, table, partner, offset, count):
    return pl.pallas_call(
        near_kernel,
        out_shape=jax.ShapeDtypeStruct((2, 3, 16, 256), jnp.float32),
        in_specs=[spec(SMEM)] * 3 + [spec(pl.ANY)] * 2 + [spec(VMEM)],
        out_specs=spec(VMEM),
        scratch_shapes=[pltpu.VMEM((2, 576, 128), jnp.float32), pltpu.SemaphoreType.DMA((2,))],
        compiler_params=PARAMS,
    )(partner, offset, count, pair, sides, table)


def far_translate(other, table, part, partner, offset, count):
    return pl.pallas_call(
        far_kernel,
        out_shape=jax.ShapeDtypeStruct((2, 3, 16, 256), jnp.float32),
        in_specs=[spec(SMEM)] * 3 + [spec(VMEM)] * 3,
        out_specs=spec(VMEM),
        compiler_params=PARAMS,
    )(partner, offset, count, other, table, part)


def shards(
    fine_pattern,
    fine_partner,
    fine_offset,
    fine_count,
    coarse_partner,
    coarse_offset,
    coarse_count,
    fine_table,
    coarse_table,
    theta_start,
    theta_weight,
    phi_interp,
    shift_phase,
):
    pattern = fine_pattern.reshape(2, 192, 128)
    inner = swap_cores(pattern)
    outer = swap_chips(pattern, 1, 1)
    even, odd = rims(pattern, inner)
    even, odd = swap_rims(even, 0), swap_rims(odd, 1)
    mats = matrices(theta_start, theta_weight, phi_interp)
    phase = shift_phase.reshape(128, 256)
    even, odd, outer = lax.optimization_barrier((even, odd, outer))
    pair = aggregate(pattern, inner, even, odd, mats, jnp.cos(phase), jnp.sin(phase))
    distant, next_to = swap_chips(pair, 1, 2), swap_chips(pair, 1, 1)
    fine_incoming = fine_translate(
        pattern, inner, outer, fine_table, fine_partner, fine_offset, fine_count
    )
    distant, next_to, fine_incoming = lax.optimization_barrier((distant, next_to, fine_incoming))
    sides = jnp.concatenate([distant, next_to], axis=1)
    other = swap_cores(sides)
    part = near_translate(pair, sides, coarse_table, coarse_partner, coarse_offset, coarse_count)
    coarse_incoming = far_translate(
        other, coarse_table, part, coarse_partner, coarse_offset, coarse_count
    )
    return (fine_incoming, coarse_incoming)


def solution(mesh):
    return jax.shard_map(
        shards,
        mesh=mesh,
        in_specs=(
            P(None, "box", "samp", None),
            P("box", None),
            P("box", None),
            P("box"),
            P("box", None),
            P("box", None),
            P("box"),
            P(None, None, "samp", None),
            P(None, None, "samp", None),
            P("samp"),
            P("samp", None),
            P(),
            P(None, "samp", None),
        ),
        out_specs=(P(None, "box", "samp", None), P(None, "box", "samp", None)),
        check_vma=False,
    )
```

```python
import functools

import jax
import jax.numpy as jnp
from jax import lax
from jax.experimental import pallas as pl
from jax.experimental.pallas import tpu as pltpu
from jax.sharding import PartitionSpec as P

VMEM = pltpu.VMEM
SMEM = pltpu.SMEM
PARAMS = pltpu.CompilerParams(vmem_limit_bytes=16 * 1024 * 1024)


def spec(space):
    return pl.BlockSpec(memory_space=space)


def matched(x, axis, pairs):
    return lax.ppermute(x, axis, pairs + [(j, i) for i, j in pairs])


def swap_cores(x):
    n = lax.axis_size("box")
    return matched(x, "box", [(i, i + 1) for i in range(0, n, 2)])


def swap_chips(x, core, distance):
    n = lax.axis_size("box")
    pairs = [(i + core, i + 2 * distance + 1 - core) for i in range(0, n - 2 * distance, 2)]
    return matched(x, "box", pairs)


def swap_rims(x, start):
    n = lax.axis_size("samp")
    return matched(x, "samp", [(i, i + 1) for i in range(start, n - 1, 2)])


def rim_kernel(own_ref, inner_ref, even_ref, odd_ref):
    odd = lax.rem(lax.axis_index("samp"), 2) == 1
    for x in range(2):
        for row in range(2):
            for which, ref in enumerate((own_ref, inner_ref)):
                first = ref[x, pl.ds(row, 24, stride=8), :]
                last = ref[x, pl.ds(6 + row, 24, stride=8), :]
                boxes = pl.ds(24 * which, 24)
                even_ref[x, row, boxes] = jnp.where(odd, first, last)
                odd_ref[x, row, boxes] = jnp.where(odd, last, first)


def rims(own, inner):
    shape = jax.ShapeDtypeStruct((2, 2, 48, 128), jnp.float32)
    return pl.pallas_call(
        rim_kernel,
        out_shape=(shape, shape),
        in_specs=[spec(VMEM)] * 2,
        out_specs=(spec(VMEM), spec(VMEM)),
        compiler_params=PARAMS,
    )(own, inner)


def split(x):
    high = x.astype(jnp.bfloat16)
    return high, (x - high.astype(jnp.float32)).astype(jnp.bfloat16)


def dot(x, y):
    return jnp.dot(x, y, preferred_element_type=jnp.float32)


SINE = (-1 / 6, 1 / 120, -1 / 5040, 1 / 362880, -1 / 39916800, 1 / 6227020800)
COSINE = (-1 / 2, 1 / 24, -1 / 720, 1 / 40320, -1 / 3628800, 1 / 479001600)


def series(square, terms):
    total = square * terms[-1]
    for term in terms[-2::-1]:
        total = square * (total + term)
    return total + 1.0


def prepare_kernel(
    start,
    weight,
    pattern,
    phi,
    phase,
    own_ref,
    theta_ref,
    theta_low_ref,
    phi_out_ref,
    phi_low_ref,
    cos_ref,
    sin_ref,
    phi_ref,
    start_ref,
    weight_ref,
    sems,
):
    copies = [
        pltpu.make_async_copy(phi, phi_ref, sems.at[0]),
        pltpu.make_async_copy(phase, sin_ref, sems.at[1]),
        pltpu.make_async_copy(pattern, own_ref, sems.at[2]),
        pltpu.make_async_copy(start, start_ref, sems.at[3]),
        pltpu.make_async_copy(weight, weight_ref, sems.at[4]),
    ]
    for copy in copies[3:] + copies[:3]:
        copy.start()
    copies[3].wait()
    copies[4].wait()
    samp = lax.axis_index("samp")
    line = lax.broadcasted_iota(jnp.int32, (16, 96), 0)
    column = lax.broadcasted_iota(jnp.int32, (16, 96), 1)
    rim = (column - 64) // 8
    rim = jnp.where((rim < 2) == (lax.rem(samp, 2) == 1), rim % 2 - 2, rim % 2 + 8)
    row = jnp.where(column < 64, column % 8, rim) + samp * 8
    theta = jnp.zeros((16, 96), jnp.float32)
    for i in range(16):
        for q in range(4):
            theta = theta + jnp.where((row == start_ref[i] + q) & (line == i), weight_ref[q, i], 0.0)
    theta = jnp.concatenate([theta] * 8, axis=0)
    line = lax.broadcasted_iota(jnp.int32, (128, 96), 0)
    column = lax.broadcasted_iota(jnp.int32, (128, 96), 1)
    child = jnp.where(column < 64, column // 8, column % 8)
    theta = jnp.where(child == line // 16, theta, 0.0)
    high, low = split(theta)
    theta_ref[...] = jnp.concatenate([high, high], axis=1)
    theta_low_ref[...] = low
    copies[0].wait()
    high, low = split(phi_ref[...].T)
    phi_out_ref[...] = jnp.concatenate([high, high], axis=0)
    phi_low_ref[...] = low
    copies[1].wait()
    half = sin_ref[...] * 0.5
    square = half * half
    sine = half * series(square, SINE)
    cos_ref[...] = 1.0 - 2.0 * sine * sine
    sin_ref[...] = 2.0 * sine * series(square, COSINE)
    copies[2].wait()


def prepare(pattern, start, weight, phi, phase):
    half, full = jnp.bfloat16, jnp.float32
    shapes = (
        ((2, 192, 128), full),
        ((128, 192), half),
        ((128, 96), half),
        ((256, 256), half),
        ((128, 256), half),
        ((128, 256), full),
        ((128, 256), full),
    )
    return pl.pallas_call(
        prepare_kernel,
        out_shape=tuple(jax.ShapeDtypeStruct(*s) for s in shapes),
        in_specs=[spec(pl.ANY)] * 5,
        out_specs=(spec(VMEM),) * 7,
        scratch_shapes=[
            pltpu.VMEM((256, 128), jnp.float32),
            pltpu.SMEM((16,), jnp.int32),
            pltpu.SMEM((4, 16), jnp.float32),
            pltpu.SemaphoreType.DMA((5,)),
        ],
        compiler_params=PARAMS,
    )(*(pltpu.with_memory_space_constraint(x, pltpu.HBM) for x in (start, weight.T, pattern, phi, phase)))


def aggregate_kernel(
    own_ref, inner_ref, even_ref, odd_ref, theta_ref, theta_low_ref, phi_ref, phi_low_ref, cos_ref, sin_ref, pair_ref
):
    me = lax.rem(lax.axis_index("box"), 2)
    theta, theta_low = theta_ref[...], theta_low_ref[...]
    phi, phi_low = phi_ref[...], phi_low_ref[...]
    for which, ref in enumerate((own_ref, inner_ref)):
        place = 96 * (me if which == 0 else 1 - me)
        for k in range(3):
            columns = []
            for x in range(2):
                parts = [ref[x, 64 * k : 64 * k + 64]]
                for rim_ref in (even_ref, odd_ref):
                    parts += [rim_ref[x, r, pl.ds(24 * which + 8 * k, 8)] for r in range(2)]
                columns.append(jnp.concatenate(parts, axis=0))
            high, low = split(jnp.concatenate(columns, axis=1))
            narrow = dot(theta, jnp.concatenate([high, low], axis=0)) + dot(theta_low, high)
            high, low = split(narrow)
            wide = []
            for x in range(2):
                part = slice(128 * x, 128 * x + 128)
                both = jnp.concatenate([high[:, part], low[:, part]], axis=1)
                wide.append(dot(both, phi) + dot(high[:, part], phi_low))
            cosine, sine = cos_ref[...], sin_ref[...]
            real_part = (cosine * wide[0] - sine * wide[1]).reshape(8, 16, 256)
            imag_part = (cosine * wide[1] + sine * wide[0]).reshape(8, 16, 256)
            for x, value in enumerate((real_part, imag_part)):
                value = jnp.sum(value, axis=0)
                for half in range(2):
                    rows = pl.ds(pl.multiple_of(place + 32 * k + 16 * half, 16), 16)
                    pair_ref[x, rows] = value[:, 128 * half : 128 * half + 128]


def aggregate(own, inner, even, odd, mats):
    return pl.pallas_call(
        aggregate_kernel,
        out_shape=jax.ShapeDtypeStruct((2, 192, 128), jnp.float32),
        in_specs=[spec(VMEM)] * 10,
        out_specs=spec(VMEM),
        compiler_params=PARAMS,
    )(own, inner, even, odd, *mats)


def fine_kernel(partner_ref, offset_ref, count_ref, own, inner, outer, table, out_ref, window, operators, sems):
    me = lax.axis_index("box")
    odd = lax.rem(me, 2)
    copies = [
        pltpu.make_async_copy(own, window.at[:, pl.ds(192, 192)], sems.at[0]),
        pltpu.make_async_copy(inner, window.at[:, pl.ds(384 * (1 - odd), 192)], sems.at[1]),
        pltpu.make_async_copy(outer, window.at[:, pl.ds(384 * odd, 192)], sems.at[2]),
        pltpu.make_async_copy(table, operators.at[:, pl.ds(0, 128)], sems.at[3]),
    ]
    for copy in copies:
        copy.start()
    operators[:, 128:] = jnp.zeros((2, 8, 128), jnp.float32)
    for copy in copies:
        copy.wait()
    base = (me - 1) * 24

    def step(b, carry):
        sums = None
        for j in range(16):
            place = pl.multiple_of((partner_ref[b, j] - base) * 8, 8)
            which = pl.multiple_of(jnp.where(j < count_ref[b], offset_ref[b, j], 16) * 8, 8)
            a, c = operators[0, pl.ds(which, 8)], operators[1, pl.ds(which, 8)]
            f, g = window[0, pl.ds(place, 8)], window[1, pl.ds(place, 8)]
            terms = (a * f, c * g, a * g, c * f)
            sums = terms if sums is None else tuple(s + t for s, t in zip(sums, terms))
        out_ref[0, b] = sums[0] - sums[1]
        out_ref[1, b] = sums[2] + sums[3]
        return carry

    lax.fori_loop(0, 24, step, 0)


def fine_translate(pattern, inner, outer, table, partner, offset, count):
    return pl.pallas_call(
        fine_kernel,
        out_shape=jax.ShapeDtypeStruct((2, 24, 8, 128), jnp.float32),
        in_specs=[spec(SMEM)] * 3 + [spec(pl.ANY)] * 4,
        out_specs=spec(VMEM),
        scratch_shapes=[
            pltpu.VMEM((2, 576, 128), jnp.float32),
            pltpu.VMEM((2, 136, 128), jnp.float32),
            pltpu.SemaphoreType.DMA((4,)),
        ],
        compiler_params=PARAMS,
        cost_estimate=pl.CostEstimate(flops=4_000_000, bytes_accessed=40_000_000, transcendentals=0),
    )(partner, offset, count, pattern, inner, outer, table.reshape(2, 128, 128))


def coarse_codes(partner_ref, offset_ref, count_ref, b, j):
    me = lax.axis_index("box")
    odd = lax.rem(me, 2) == 1
    place = partner_ref[b, j] - (me // 2 - 2) * 6
    side = jnp.where(odd, place >= 12, place < 18)
    place = jnp.where(place >= 24, place - 24, jnp.where(place >= 18, place - 12, place))
    code = jnp.where(j < count_ref[b], place * 512 + offset_ref[b, j], -1)
    return jnp.where(side, code, -1), jnp.where(side, -1, code)


def coarse_sums(window, table, codes):
    sums = [None, None]
    for code in codes:
        scale = jnp.where(code >= 0, 1.0, 0.0)
        code = jnp.maximum(code, 0)
        which = lax.bitwise_and(code, 15)
        place = pl.multiple_of(lax.shift_right_logical(code, 4), 32)
        for half in range(2):
            lanes = slice(128 * half, 128 * half + 128)
            a, c = table[0, which, :, lanes] * scale, table[1, which, :, lanes] * scale
            f, g = window[0, pl.ds(place + 16 * half, 16)], window[1, pl.ds(place + 16 * half, 16)]
            terms = (a * f, c * g, a * g, c * f)
            old = sums[half]
            sums[half] = terms if old is None else tuple(s + t for s, t in zip(old, terms))
    return [(s[0] - s[1], s[2] + s[3]) for s in sums]


def near_kernel(partner_ref, offset_ref, count_ref, pair, sides, table, out_ref, code_ref, window, sems):
    copies = [
        pltpu.make_async_copy(sides, window.at[:, pl.ds(0, 384)], sems.at[0]),
        pltpu.make_async_copy(pair, window.at[:, pl.ds(384, 192)], sems.at[1]),
    ]
    for copy in copies:
        copy.start()
    for copy in copies:
        copy.wait()

    def step(b, carry):
        codes = []
        for j in range(16):
            near, far = coarse_codes(partner_ref, offset_ref, count_ref, b, j)
            codes.append(near)
            code_ref[b, j] = far
        sums = coarse_sums(window, table, codes)
        for half in range(2):
            for x in range(2):
                out_ref[x, b, :, 128 * half : 128 * half + 128] = sums[half][x]
        return carry

    lax.fori_loop(0, 3, step, 0)


def far_kernel(code_ref, other, table, part_ref, out_ref):
    def step(b, carry):
        sums = coarse_sums(other, table, [code_ref[b, j] for j in range(16)])
        for half in range(2):
            lanes = slice(128 * half, 128 * half + 128)
            for x in range(2):
                out_ref[x, b, :, lanes] = part_ref[x, b, :, lanes] + sums[half][x]
        return carry

    lax.fori_loop(0, 3, step, 0)


def near_translate(pair, sides, table, partner, offset, count):
    return pl.pallas_call(
        near_kernel,
        out_shape=(
            jax.ShapeDtypeStruct((2, 3, 16, 256), jnp.float32),
            jax.ShapeDtypeStruct((3, 16), jnp.int32),
        ),
        in_specs=[spec(SMEM)] * 3 + [spec(pl.ANY)] * 2 + [spec(VMEM)],
        out_specs=(spec(VMEM), spec(SMEM)),
        scratch_shapes=[pltpu.VMEM((2, 576, 128), jnp.float32), pltpu.SemaphoreType.DMA((2,))],
        compiler_params=PARAMS,
    )(partner, offset, count, pair, sides, table)


def far_translate(other, table, part, codes):
    return pl.pallas_call(
        far_kernel,
        out_shape=jax.ShapeDtypeStruct((2, 3, 16, 256), jnp.float32),
        in_specs=[spec(SMEM)] + [spec(VMEM)] * 3,
        out_specs=spec(VMEM),
        compiler_params=PARAMS,
    )(codes, other, table, part)


def shards(
    fine_pattern,
    fine_partner,
    fine_offset,
    fine_count,
    coarse_partner,
    coarse_offset,
    coarse_count,
    fine_table,
    coarse_table,
    theta_start,
    theta_weight,
    phi_interp,
    shift_phase,
):
    pattern = fine_pattern.reshape(2, 192, 128)
    inner = swap_cores(pattern)
    own, *mats = prepare(pattern, theta_start, theta_weight, phi_interp, shift_phase.reshape(128, 256))
    inner, own, mats = lax.optimization_barrier((inner, own, mats))
    even, odd = rims(own, inner)
    even, odd, late = lax.optimization_barrier((even, odd, own))
    outer = swap_chips(late, 1, 1)
    even, odd = swap_rims(even, 0), swap_rims(odd, 1)
    pair = aggregate(own, inner, even, odd, mats)
    distant, next_to = swap_chips(pair, 1, 2), swap_chips(pair, 1, 1)
    fine_incoming = fine_translate(
        own, inner, outer, fine_table, fine_partner, fine_offset, fine_count
    )
    distant, next_to, fine_incoming = lax.optimization_barrier((distant, next_to, fine_incoming))
    sides = jnp.concatenate([distant, next_to], axis=1)
    other = swap_cores(sides)
    part, codes = near_translate(
        pair, sides, coarse_table, coarse_partner, coarse_offset, coarse_count
    )
    coarse_incoming = far_translate(other, coarse_table, part, codes)
    return (fine_incoming, coarse_incoming)


def solution(mesh):
    return jax.shard_map(
        shards,
        mesh=mesh,
        in_specs=(
            P(None, "box", "samp", None),
            P("box", None),
            P("box", None),
            P("box"),
            P("box", None),
            P("box", None),
            P("box"),
            P(None, None, "samp", None),
            P(None, None, "samp", None),
            P("samp"),
            P("samp", None),
            P(),
            P(None, "samp", None),
        ),
        out_specs=(P(None, "box", "samp", None), P(None, "box", "samp", None)),
        check_vma=False,
    )
```

```python
import functools

import jax
import jax.numpy as jnp
from jax import lax
from jax.experimental import pallas as pl
from jax.experimental.pallas import tpu as pltpu
from jax.sharding import PartitionSpec as P

VMEM = pltpu.VMEM
SMEM = pltpu.SMEM
PARAMS = pltpu.CompilerParams(vmem_limit_bytes=16 * 1024 * 1024)


def spec(space):
    return pl.BlockSpec(memory_space=space)


def matched(x, axis, pairs):
    return lax.ppermute(x, axis, pairs + [(j, i) for i, j in pairs])


def swap_cores(x):
    n = lax.axis_size("box")
    return matched(x, "box", [(i, i + 1) for i in range(0, n, 2)])


def swap_chips(x, core, distance):
    n = lax.axis_size("box")
    pairs = [(i + core, i + 2 * distance + 1 - core) for i in range(0, n - 2 * distance, 2)]
    return matched(x, "box", pairs)


def swap_rims(x, start):
    n = lax.axis_size("samp")
    return matched(x, "samp", [(i, i + 1) for i in range(start, n - 1, 2)])


def rim_kernel(own_ref, inner_ref, even_ref, odd_ref):
    odd = lax.rem(lax.axis_index("samp"), 2) == 1
    for x in range(2):
        for row in range(2):
            for which, ref in enumerate((own_ref, inner_ref)):
                first = ref[x, pl.ds(row, 24, stride=8), :]
                last = ref[x, pl.ds(6 + row, 24, stride=8), :]
                boxes = pl.ds(24 * which, 24)
                even_ref[x, row, boxes] = jnp.where(odd, first, last)
                odd_ref[x, row, boxes] = jnp.where(odd, last, first)


def rims(own, inner):
    shape = jax.ShapeDtypeStruct((2, 2, 48, 128), jnp.float32)
    return pl.pallas_call(
        rim_kernel,
        out_shape=(shape, shape),
        in_specs=[spec(VMEM)] * 2,
        out_specs=(spec(VMEM), spec(VMEM)),
        compiler_params=PARAMS,
    )(own, inner)


def split(x):
    high = x.astype(jnp.bfloat16)
    return high, (x - high.astype(jnp.float32)).astype(jnp.bfloat16)


def dot(x, y):
    return jnp.dot(x, y, preferred_element_type=jnp.float32)


SINE = (-1 / 6, 1 / 120, -1 / 5040, 1 / 362880, -1 / 39916800, 1 / 6227020800)
COSINE = (-1 / 2, 1 / 24, -1 / 720, 1 / 40320, -1 / 3628800, 1 / 479001600)


def series(square, terms):
    total = square * terms[-1]
    for term in terms[-2::-1]:
        total = square * (total + term)
    return total + 1.0


def prepare_kernel(
    start,
    weight,
    pattern,
    phi,
    phase,
    own_ref,
    theta_ref,
    theta_low_ref,
    phi_out_ref,
    phi_low_ref,
    cos_ref,
    sin_ref,
    phi_ref,
    start_ref,
    weight_ref,
    sems,
):
    copies = [
        pltpu.make_async_copy(phi, phi_ref, sems.at[0]),
        pltpu.make_async_copy(phase, sin_ref, sems.at[1]),
        pltpu.make_async_copy(pattern, own_ref, sems.at[2]),
        pltpu.make_async_copy(start, start_ref, sems.at[3]),
        pltpu.make_async_copy(weight, weight_ref, sems.at[4]),
    ]
    for copy in copies[3:] + copies[:3]:
        copy.start()
    copies[3].wait()
    copies[4].wait()
    samp = lax.axis_index("samp")
    line = lax.broadcasted_iota(jnp.int32, (16, 96), 0)
    column = lax.broadcasted_iota(jnp.int32, (16, 96), 1)
    rim = (column - 64) // 8
    rim = jnp.where((rim < 2) == (lax.rem(samp, 2) == 1), rim % 2 - 2, rim % 2 + 8)
    row = jnp.where(column < 64, column % 8, rim) + samp * 8
    theta = jnp.zeros((16, 96), jnp.float32)
    for i in range(16):
        for q in range(4):
            theta = theta + jnp.where((row == start_ref[i] + q) & (line == i), weight_ref[q, i], 0.0)
    theta = jnp.concatenate([theta] * 8, axis=0)
    line = lax.broadcasted_iota(jnp.int32, (128, 96), 0)
    column = lax.broadcasted_iota(jnp.int32, (128, 96), 1)
    child = jnp.where(column < 64, column // 8, column % 8)
    theta = jnp.where(child == line // 16, theta, 0.0)
    high, low = split(theta)
    theta_ref[...] = jnp.concatenate([high, high], axis=1)
    theta_low_ref[...] = low
    copies[0].wait()
    high, low = split(phi_ref[...].T)
    phi_out_ref[...] = jnp.concatenate([high, high], axis=0)
    phi_low_ref[...] = low
    copies[1].wait()
    half = sin_ref[...] * 0.5
    square = half * half
    sine = half * series(square, SINE)
    cos_ref[...] = 1.0 - 2.0 * sine * sine
    sin_ref[...] = 2.0 * sine * series(square, COSINE)
    copies[2].wait()


def prepare(pattern, start, weight, phi, phase):
    half, full = jnp.bfloat16, jnp.float32
    shapes = (
        ((2, 192, 128), full),
        ((128, 192), half),
        ((128, 96), half),
        ((256, 256), half),
        ((128, 256), half),
        ((128, 256), full),
        ((128, 256), full),
    )
    return pl.pallas_call(
        prepare_kernel,
        out_shape=tuple(jax.ShapeDtypeStruct(*s) for s in shapes),
        in_specs=[spec(pl.ANY)] * 5,
        out_specs=(spec(VMEM),) * 7,
        scratch_shapes=[
            pltpu.VMEM((256, 128), jnp.float32),
            pltpu.SMEM((16,), jnp.int32),
            pltpu.SMEM((4, 16), jnp.float32),
            pltpu.SemaphoreType.DMA((5,)),
        ],
        compiler_params=PARAMS,
    )(*in_hbm(start, weight.T, pattern, phi, phase))


def aggregate_kernel(
    own_ref, inner_ref, even_ref, odd_ref, theta_ref, theta_low_ref, phi_ref, phi_low_ref, cos_ref, sin_ref, pair_ref
):
    me = lax.rem(lax.axis_index("box"), 2)
    theta, theta_low = theta_ref[...], theta_low_ref[...]
    phi, phi_low = phi_ref[...], phi_low_ref[...]
    for which, ref in enumerate((own_ref, inner_ref)):
        place = 96 * (me if which == 0 else 1 - me)
        for k in range(3):
            columns = []
            for x in range(2):
                parts = [ref[x, 64 * k : 64 * k + 64]]
                for rim_ref in (even_ref, odd_ref):
                    parts += [rim_ref[x, r, pl.ds(24 * which + 8 * k, 8)] for r in range(2)]
                columns.append(jnp.concatenate(parts, axis=0))
            high, low = split(jnp.concatenate(columns, axis=1))
            narrow = dot(theta, jnp.concatenate([high, low], axis=0)) + dot(theta_low, high)
            high, low = split(narrow)
            wide = []
            for x in range(2):
                part = slice(128 * x, 128 * x + 128)
                both = jnp.concatenate([high[:, part], low[:, part]], axis=1)
                wide.append(dot(both, phi) + dot(high[:, part], phi_low))
            cosine, sine = cos_ref[...], sin_ref[...]
            real_part = (cosine * wide[0] - sine * wide[1]).reshape(8, 16, 256)
            imag_part = (cosine * wide[1] + sine * wide[0]).reshape(8, 16, 256)
            for x, value in enumerate((real_part, imag_part)):
                value = jnp.sum(value, axis=0)
                for half in range(2):
                    rows = pl.ds(pl.multiple_of(place + 32 * k + 16 * half, 16), 16)
                    pair_ref[x, rows] = value[:, 128 * half : 128 * half + 128]


def aggregate(own, inner, even, odd, mats):
    return pl.pallas_call(
        aggregate_kernel,
        out_shape=jax.ShapeDtypeStruct((2, 192, 128), jnp.float32),
        in_specs=[spec(VMEM)] * 10,
        out_specs=spec(VMEM),
        compiler_params=PARAMS,
    )(own, inner, even, odd, *mats)


def fine_kernel(
    partner,
    offset,
    count,
    table,
    own,
    inner,
    outer,
    out,
    window,
    operators,
    value_ref,
    partner_ref,
    offset_ref,
    count_ref,
    sems,
    out_sems,
):
    me = lax.axis_index("box")
    odd = lax.rem(me, 2)
    moves = (
        (partner, partner_ref),
        (offset, offset_ref),
        (count, count_ref),
        (table, operators.at[:, pl.ds(0, 128)]),
        (own, window.at[:, pl.ds(192, 192)]),
        (inner, window.at[:, pl.ds(384 * (1 - odd), 192)]),
        (outer, window.at[:, pl.ds(384 * odd, 192)]),
    )
    copies = [pltpu.make_async_copy(*move, sems.at[i]) for i, move in enumerate(moves)]
    for copy in copies:
        copy.start()
    operators[:, 128:] = jnp.zeros((2, 8, 128), jnp.float32)
    for copy in copies:
        copy.wait()
    base = (me - 1) * 24

    def step(b, carry):
        sums = None
        for j in range(16):
            place = pl.multiple_of((partner_ref[j, b] - base) * 8, 8)
            which = pl.multiple_of(jnp.where(j < count_ref[b], offset_ref[j, b], 16) * 8, 8)
            a, c = operators[0, pl.ds(which, 8)], operators[1, pl.ds(which, 8)]
            f, g = window[0, pl.ds(place, 8)], window[1, pl.ds(place, 8)]
            terms = (a * f, c * g, a * g, c * f)
            sums = terms if sums is None else tuple(s + t for s, t in zip(sums, terms))
        value_ref[0, b] = sums[0] - sums[1]
        value_ref[1, b] = sums[2] + sums[3]
        return carry

    copies = []
    for part in range(3):
        lax.fori_loop(8 * part, 8 * part + 8, step, 0)
        boxes = pl.ds(8 * part, 8)
        copies.append(pltpu.make_async_copy(value_ref.at[:, boxes], out.at[:, boxes], out_sems.at[part]))
        copies[part].start()
    for copy in copies:
        copy.wait()


def in_hbm(*arrays):
    return tuple(pltpu.with_memory_space_constraint(x, pltpu.HBM) for x in arrays)


def fine_translate(pattern, inner, outer, table, partner, offset, count):
    return pl.pallas_call(
        fine_kernel,
        out_shape=jax.ShapeDtypeStruct((2, 24, 8, 128), jnp.float32),
        in_specs=[spec(pl.ANY)] * 7,
        out_specs=spec(pl.ANY),
        scratch_shapes=[
            pltpu.VMEM((2, 576, 128), jnp.float32),
            pltpu.VMEM((2, 136, 128), jnp.float32),
            pltpu.VMEM((2, 24, 8, 128), jnp.float32),
            pltpu.SMEM((16, 24), jnp.int32),
            pltpu.SMEM((16, 24), jnp.int32),
            pltpu.SMEM((24,), jnp.int32),
            pltpu.SemaphoreType.DMA((7,)),
            pltpu.SemaphoreType.DMA((3,)),
        ],
        compiler_params=PARAMS,
        cost_estimate=pl.CostEstimate(flops=4_000_000, bytes_accessed=4_000_000, transcendentals=0),
    )(*in_hbm(partner.T, offset.T, count, table.reshape(2, 128, 128)), pattern, inner, outer)


def coarse_box(b, partner_ref, offset_ref, count_ref):
    base = (lax.axis_index("box") // 2 - 2) * 6
    return [(j < count_ref[b], partner_ref[b, j] - base, offset_ref[b, j]) for j in range(16)]


def coarse_sums(window, table, slots):
    sums = [None, None]
    for live, place, which in slots:
        place = pl.multiple_of(jnp.where(live, place, 0) * 32, 32)
        scale = jnp.where(live, 1.0, 0.0)
        for half in range(2):
            lanes = slice(128 * half, 128 * half + 128)
            rows = pl.ds(place + 16 * half, 16)
            a, c = table[0, which, :, lanes] * scale, table[1, which, :, lanes] * scale
            f, g = window[0, rows], window[1, rows]
            terms = (a * f, c * g, a * g, c * f)
            old = sums[half]
            sums[half] = terms if old is None else tuple(s + t for s, t in zip(old, terms))
    return [(s[0] - s[1], s[2] + s[3]) for s in sums]


def first_kernel(partner_ref, offset_ref, count_ref, table, pair_ref, out_ref, dense_ref):
    odd = lax.rem(lax.axis_index("box"), 2) == 1
    dense_ref[...] = jnp.zeros(dense_ref.shape, jnp.float32)

    def step(b, carry):
        slots = []
        for live, box, which in coarse_box(b, partner_ref, offset_ref, count_ref):
            far = jnp.logical_and(live, jnp.where(odd, box < 12, box >= 18))
            place = jnp.where(odd, jnp.where(box >= 6, box - 6, box + 6), box - 18)
            row = pl.multiple_of(jnp.where(far, b * 12 + place, 36) * 16, 16)
            for x in range(2):
                dense_ref[x, pl.ds(row, 16)] = table[x, which]
            slots.append((live & (box >= 12) & (box < 18), box - 12, which))
        sums = coarse_sums(pair_ref, table, slots)
        for half in range(2):
            for x in range(2):
                out_ref[x, b, :, 128 * half : 128 * half + 128] = sums[half][x]
        return carry

    lax.fori_loop(0, 3, step, 0)


def second_kernel(partner_ref, offset_ref, count_ref, table, sides_ref, part_ref, out_ref):
    odd = lax.rem(lax.axis_index("box"), 2) == 1

    def step(b, carry):
        slots = []
        for live, box, which in coarse_box(b, partner_ref, offset_ref, count_ref):
            place = jnp.where(odd, box - 18, jnp.where(box >= 6, box - 6, box + 6))
            slots.append((jnp.logical_and(live, jnp.where(odd, box >= 18, box < 12)), place, which))
        sums = coarse_sums(sides_ref, table, slots)
        for half in range(2):
            lanes = slice(128 * half, 128 * half + 128)
            for x in range(2):
                out_ref[x, b, :, lanes] = part_ref[x, b, :, lanes] + sums[half][x]
        return carry

    lax.fori_loop(0, 3, step, 0)


def far_kernel(other, dense, part, out, value_ref, sems):
    copies = []
    for half in range(2):
        for top in (0, 8):
            lanes, lines = pl.ds(128 * half, 128), pl.ds(top, 8)
            sums = [(part[0, b, lines, lanes], part[1, b, lines, lanes]) for b in range(3)]
            for s in range(12):
                rows = pl.ds(32 * s + 16 * half + top, 8)
                f, g = other[0, rows], other[1, rows]
                for b in range(3):
                    places = pl.ds((12 * b + s) * 16 + top, 8)
                    a, c = dense[0, places, lanes], dense[1, places, lanes]
                    sums[b] = (sums[b][0] + (a * f - c * g), sums[b][1] + (a * g + c * f))
            for b in range(3):
                for x in range(2):
                    value_ref[x, b, lines, lanes] = sums[b][x]
            copies.append(
                pltpu.make_async_copy(
                    value_ref.at[:, :, lines, lanes], out.at[:, :, lines, lanes], sems.at[len(copies)]
                )
            )
            copies[-1].start()
    for copy in copies:
        copy.wait()


def first_translate(lists, table, pair):
    return pl.pallas_call(
        first_kernel,
        out_shape=(
            jax.ShapeDtypeStruct((2, 3, 16, 256), jnp.float32),
            jax.ShapeDtypeStruct((2, 37 * 16, 256), jnp.float32),
        ),
        in_specs=[spec(SMEM)] * 3 + [spec(VMEM)] * 2,
        out_specs=(spec(VMEM), spec(VMEM)),
        compiler_params=PARAMS,
    )(*lists, table, pair)


def second_translate(lists, table, sides, part):
    return pl.pallas_call(
        second_kernel,
        out_shape=jax.ShapeDtypeStruct((2, 3, 16, 256), jnp.float32),
        in_specs=[spec(SMEM)] * 3 + [spec(VMEM)] * 3,
        out_specs=spec(VMEM),
        compiler_params=PARAMS,
    )(*lists, table, sides, part)


def far_translate(other, dense, part):
    return pl.pallas_call(
        far_kernel,
        out_shape=jax.ShapeDtypeStruct((2, 3, 16, 256), jnp.float32),
        in_specs=[spec(VMEM)] * 3,
        out_specs=spec(pl.ANY),
        scratch_shapes=[pltpu.VMEM((2, 3, 16, 256), jnp.float32), pltpu.SemaphoreType.DMA((4,))],
        compiler_params=PARAMS,
    )(other, dense, part)


def shards(
    fine_pattern,
    fine_partner,
    fine_offset,
    fine_count,
    coarse_partner,
    coarse_offset,
    coarse_count,
    fine_table,
    coarse_table,
    theta_start,
    theta_weight,
    phi_interp,
    shift_phase,
):
    pattern = fine_pattern.reshape(2, 192, 128)
    inner = swap_cores(pattern)
    own, *mats = prepare(pattern, theta_start, theta_weight, phi_interp, shift_phase.reshape(128, 256))
    inner, own, mats = lax.optimization_barrier((inner, own, mats))
    even, odd = rims(own, inner)
    even, odd, late = lax.optimization_barrier((even, odd, own))
    outer = swap_chips(late, 1, 1)
    even, odd = swap_rims(even, 0), swap_rims(odd, 1)
    pair = aggregate(own, inner, even, odd, mats)
    next_to, distant = swap_chips(pair, 1, 1), swap_chips(pair, 1, 2)
    fine_incoming = fine_translate(
        own, inner, outer, fine_table, fine_partner, fine_offset, fine_count
    )
    lists = (coarse_partner, coarse_offset, coarse_count)
    part, dense = first_translate(lists, coarse_table, pair)
    distant, fine_incoming, part, dense = lax.optimization_barrier((distant, fine_incoming, part, dense))
    next_to, distant = lax.optimization_barrier((next_to, distant))
    sides = jnp.concatenate([next_to, distant], axis=1)
    other = swap_cores(sides)
    part = second_translate(lists, coarse_table, sides, part)
    coarse_incoming = far_translate(other, dense, part)
    return (fine_incoming, coarse_incoming)


def solution(mesh):
    return jax.shard_map(
        shards,
        mesh=mesh,
        in_specs=(
            P(None, "box", "samp", None),
            P("box", None),
            P("box", None),
            P("box"),
            P("box", None),
            P("box", None),
            P("box"),
            P(None, None, "samp", None),
            P(None, None, "samp", None),
            P("samp"),
            P("samp", None),
            P(),
            P(None, "samp", None),
        ),
        out_specs=(P(None, "box", "samp", None), P(None, "box", "samp", None)),
        check_vma=False,
    )
```

```python
import functools

import jax
import jax.numpy as jnp
from jax import lax
from jax.experimental import pallas as pl
from jax.experimental.pallas import tpu as pltpu
from jax.sharding import PartitionSpec as P

VMEM = pltpu.VMEM
SMEM = pltpu.SMEM
PARAMS = pltpu.CompilerParams(vmem_limit_bytes=16 * 1024 * 1024)


def spec(space):
    return pl.BlockSpec(memory_space=space)


def matched(x, axis, pairs):
    return lax.ppermute(x, axis, pairs + [(j, i) for i, j in pairs])


def swap_cores(x):
    n = lax.axis_size("box")
    return matched(x, "box", [(i, i + 1) for i in range(0, n, 2)])


def swap_chips(x, core, distance):
    n = lax.axis_size("box")
    pairs = [(i + core, i + 2 * distance + 1 - core) for i in range(0, n - 2 * distance, 2)]
    return matched(x, "box", pairs)


def swap_rims(x, start):
    n = lax.axis_size("samp")
    return matched(x, "samp", [(i, i + 1) for i in range(start, n - 1, 2)])


def rim_kernel(own_ref, inner_ref, even_ref, odd_ref):
    odd = lax.rem(lax.axis_index("samp"), 2) == 1
    for x in range(2):
        for row in range(2):
            for which, ref in enumerate((own_ref, inner_ref)):
                first = ref[x, pl.ds(row, 24, stride=8), :]
                last = ref[x, pl.ds(6 + row, 24, stride=8), :]
                boxes = pl.ds(24 * which, 24)
                even_ref[x, row, boxes] = jnp.where(odd, first, last)
                odd_ref[x, row, boxes] = jnp.where(odd, last, first)


def rims(own, inner):
    shape = jax.ShapeDtypeStruct((2, 2, 48, 128), jnp.float32)
    return pl.pallas_call(
        rim_kernel,
        out_shape=(shape, shape),
        in_specs=[spec(VMEM)] * 2,
        out_specs=(spec(VMEM), spec(VMEM)),
        compiler_params=PARAMS,
    )(own, inner)


def split(x):
    high = x.astype(jnp.bfloat16)
    return high, (x - high.astype(jnp.float32)).astype(jnp.bfloat16)


def dot(x, y):
    return jnp.dot(x, y, preferred_element_type=jnp.float32)


SINE = (-1 / 6, 1 / 120, -1 / 5040, 1 / 362880, -1 / 39916800, 1 / 6227020800)
COSINE = (-1 / 2, 1 / 24, -1 / 720, 1 / 40320, -1 / 3628800, 1 / 479001600)


def series(square, terms):
    total = square * terms[-1]
    for term in terms[-2::-1]:
        total = square * (total + term)
    return total + 1.0


def prepare_kernel(
    start,
    weight,
    pattern,
    phi,
    phase,
    own_ref,
    theta_ref,
    theta_rim_ref,
    phi_out_ref,
    phi_low_ref,
    cos_ref,
    sin_ref,
    phi_ref,
    start_ref,
    weight_ref,
    sems,
):
    copies = [
        pltpu.make_async_copy(phi, phi_ref, sems.at[0]),
        pltpu.make_async_copy(phase, sin_ref, sems.at[1]),
        pltpu.make_async_copy(pattern, own_ref, sems.at[2]),
        pltpu.make_async_copy(start, start_ref, sems.at[3]),
        pltpu.make_async_copy(weight, weight_ref, sems.at[4]),
    ]
    for copy in copies[3:] + copies[:3]:
        copy.start()
    copies[3].wait()
    copies[4].wait()
    samp = lax.axis_index("samp")
    odd = lax.rem(samp, 2)
    line = lax.broadcasted_iota(jnp.int32, (16, 80), 0)
    column = lax.broadcasted_iota(jnp.int32, (16, 80), 1)
    rim = (column - 64) // 8 + jnp.where(odd == 1, -2, 8)
    row = jnp.where(column < 64, column % 8, rim) + samp * 8
    theta = jnp.zeros((16, 80), jnp.float32)
    for i in range(16):
        for q in range(4):
            theta = theta + jnp.where((row == start_ref[i] + q) & (line == i), weight_ref[q, i], 0.0)
    theta = jnp.concatenate([theta] * 8, axis=0)
    line = lax.broadcasted_iota(jnp.int32, (128, 80), 0)
    column = lax.broadcasted_iota(jnp.int32, (128, 80), 1)
    child = jnp.where(column < 64, column // 8, column % 8)
    high, low = split(jnp.where(child == line // 16, theta, 0.0))
    theta_ref[...] = jnp.concatenate([high, high, low], axis=1)
    line = lax.broadcasted_iota(jnp.int32, (8, 32), 0)
    column = lax.broadcasted_iota(jnp.int32, (8, 32), 1)
    row = column // 8 % 2 + jnp.where(odd == 1, 8, -2) + samp * 8
    theta = jnp.zeros((8, 32), jnp.float32)
    for i in range(4):
        for q in range(4):
            near = (row == start_ref[i + 12 * odd] + q) & (line % 4 == i) & (line // 4 == column // 16)
            theta = theta + jnp.where(near, weight_ref[q, i + 12 * odd], 0.0)
    theta = jnp.concatenate([theta] * 8, axis=0)
    line = lax.broadcasted_iota(jnp.int32, (64, 32), 0)
    column = lax.broadcasted_iota(jnp.int32, (64, 32), 1)
    high, low = split(jnp.where(line // 8 == column % 8, theta, 0.0))
    theta_rim_ref[...] = jnp.concatenate([high, high, low], axis=1)
    copies[0].wait()
    high, low = split(phi_ref[...].T)
    phi_out_ref[...] = jnp.concatenate([high, high], axis=0)
    phi_low_ref[...] = low
    copies[1].wait()
    half = sin_ref[...] * 0.5
    square = half * half
    sine = half * series(square, SINE)
    cos_ref[...] = 1.0 - 2.0 * sine * sine
    sin_ref[...] = 2.0 * sine * series(square, COSINE)
    copies[2].wait()


def prepare(pattern, start, weight, phi, phase):
    half, full = jnp.bfloat16, jnp.float32
    shapes = (
        ((2, 192, 128), full),
        ((128, 240), half),
        ((64, 96), half),
        ((256, 256), half),
        ((128, 256), half),
        ((128, 256), full),
        ((128, 256), full),
    )
    return pl.pallas_call(
        prepare_kernel,
        out_shape=tuple(jax.ShapeDtypeStruct(*s) for s in shapes),
        in_specs=[spec(pl.ANY)] * 5,
        out_specs=(spec(VMEM),) * 7,
        scratch_shapes=[
            pltpu.VMEM((256, 128), jnp.float32),
            pltpu.SMEM((16,), jnp.int32),
            pltpu.SMEM((4, 16), jnp.float32),
            pltpu.SemaphoreType.DMA((5,)),
        ],
        compiler_params=PARAMS,
    )(*in_hbm(start, weight.T, pattern, phi, phase))


def terms_of(parts):
    high, low = split(jnp.concatenate([jnp.concatenate(part, axis=0) for part in parts], axis=1))
    return jnp.concatenate([high, low, high], axis=0)


def widen_and_sum(narrow, phi, phi_low, cosine, sine):
    high, low = split(narrow)
    wide = []
    for x in range(2):
        part = slice(128 * x, 128 * x + 128)
        both = jnp.concatenate([high[:, part], low[:, part]], axis=1)
        wide.append(dot(both, phi) + dot(high[:, part], phi_low))
    shape = (8, narrow.shape[0] // 8, 256)
    real_part = (cosine * wide[0] - sine * wide[1]).reshape(shape)
    imag_part = (cosine * wide[1] + sine * wide[0]).reshape(shape)
    return jnp.sum(real_part, axis=0), jnp.sum(imag_part, axis=0)


def pair_row(box):
    me = lax.rem(lax.axis_index("box"), 2)
    return 96 * (me if box < 3 else 1 - me) + 32 * (box % 3)


def aggregate_kernel(
    own_ref, inner_ref, rim_ref, theta_ref, phi_ref, phi_low_ref, cos_ref, sin_ref, pair_ref, cos_rim_ref, sin_rim_ref
):
    even = lax.rem(lax.axis_index("samp"), 2) == 0
    theta, phi, phi_low = theta_ref[...], phi_ref[...], phi_low_ref[...]
    for box in range(6):
        ref = own_ref if box < 3 else inner_ref
        k = box % 3
        parts = []
        for x in range(2):
            rows = [ref[x, 64 * k : 64 * k + 64]]
            parts.append(rows + [rim_ref[x, r, pl.ds(8 * box, 8)] for r in range(2)])
        narrow = dot(theta, terms_of(parts))
        values = widen_and_sum(narrow, phi, phi_low, cos_ref[...], sin_ref[...])
        for x in range(2):
            for half in range(2):
                rows = pl.ds(pl.multiple_of(pair_row(box) + 16 * half, 16), 16)
                pair_ref[x, rows] = values[x][:, 128 * half : 128 * half + 128]
    first = (lax.broadcasted_iota(jnp.int32, (8, 256), 0) < 4) == even
    for ref, out_ref in ((cos_ref, cos_rim_ref), (sin_ref, sin_rim_ref)):
        for child in range(8):
            rows = ref[pl.ds(pl.multiple_of(16 * child + jnp.where(even, 0, 8), 8), 8)]
            out_ref[8 * child : 8 * child + 8] = jnp.where(first, rows, pltpu.roll(rows, 4, 0))


def aggregate(own, inner, rim, theta, phi, phi_low, cosine, sine):
    waves = jax.ShapeDtypeStruct((64, 256), jnp.float32)
    return pl.pallas_call(
        aggregate_kernel,
        out_shape=(jax.ShapeDtypeStruct((2, 192, 128), jnp.float32), waves, waves),
        in_specs=[spec(VMEM)] * 8,
        out_specs=(spec(VMEM),) * 3,
        compiler_params=PARAMS,
    )(own, inner, rim, theta, phi, phi_low, cosine, sine)


def rim_sums_kernel(part_ref, rim_ref, theta_ref, phi_ref, phi_low_ref, cos_ref, sin_ref, pair_ref):
    even = lax.rem(lax.axis_index("samp"), 2) == 0
    pair_ref[...] = part_ref[...]
    upper = lax.broadcasted_iota(jnp.int32, (8, 128), 0) < 4
    theta, phi, phi_low = theta_ref[...], phi_ref[...], phi_low_ref[...]
    for group in range(3):
        boxes = (2 * group, 2 * group + 1)
        parts = [[rim_ref[x, r, pl.ds(8 * box, 8)] for box in boxes for r in range(2)] for x in range(2)]
        narrow = dot(theta, terms_of(parts))
        values = widen_and_sum(narrow, phi, phi_low, cos_ref[...], sin_ref[...])
        for x in range(2):
            for half in range(2):
                value = values[x][:, 128 * half : 128 * half + 128]
                turned = pltpu.roll(value, 4, 0)
                for order, box in enumerate(boxes):
                    rows = pl.ds(pl.multiple_of(pair_row(box) + 16 * half + jnp.where(even, 0, 8), 8), 8)
                    here = jnp.where(even, *((value, turned) if order == 0 else (turned, value)))
                    pair_ref[x, rows] += jnp.where(upper == even, here, 0.0)


def rim_sums(part, rim, theta, phi, phi_low, cosine, sine):
    return pl.pallas_call(
        rim_sums_kernel,
        out_shape=jax.ShapeDtypeStruct((2, 192, 128), jnp.float32),
        in_specs=[spec(VMEM)] * 7,
        out_specs=spec(VMEM),
        compiler_params=PARAMS,
    )(part, rim, theta, phi, phi_low, cosine, sine)


def fine_kernel(
    partner,
    offset,
    count,
    table,
    own,
    inner,
    outer,
    out,
    window,
    operators,
    value_ref,
    partner_ref,
    offset_ref,
    count_ref,
    sems,
    out_sems,
):
    me = lax.axis_index("box")
    odd = lax.rem(me, 2)
    moves = (
        (partner, partner_ref),
        (offset, offset_ref),
        (count, count_ref),
        (table, operators.at[:, pl.ds(0, 128)]),
        (own, window.at[:, pl.ds(192, 192)]),
        (inner, window.at[:, pl.ds(384 * (1 - odd), 192)]),
        (outer, window.at[:, pl.ds(384 * odd, 192)]),
    )
    copies = [pltpu.make_async_copy(*move, sems.at[i]) for i, move in enumerate(moves)]
    for copy in copies:
        copy.start()
    operators[:, 128:] = jnp.zeros((2, 8, 128), jnp.float32)
    for copy in copies:
        copy.wait()
    base = (me - 1) * 24

    def step(b, carry):
        sums = None
        for j in range(16):
            place = pl.multiple_of((partner_ref[j, b] - base) * 8, 8)
            which = pl.multiple_of(jnp.where(j < count_ref[b], offset_ref[j, b], 16) * 8, 8)
            a, c = operators[0, pl.ds(which, 8)], operators[1, pl.ds(which, 8)]
            f, g = window[0, pl.ds(place, 8)], window[1, pl.ds(place, 8)]
            terms = (a * f, c * g, a * g, c * f)
            sums = terms if sums is None else tuple(s + t for s, t in zip(sums, terms))
        value_ref[0, b] = sums[0] - sums[1]
        value_ref[1, b] = sums[2] + sums[3]
        return carry

    copies = []
    for part in range(3):
        lax.fori_loop(8 * part, 8 * part + 8, step, 0)
        boxes = pl.ds(8 * part, 8)
        copies.append(pltpu.make_async_copy(value_ref.at[:, boxes], out.at[:, boxes], out_sems.at[part]))
        copies[part].start()
    for copy in copies:
        copy.wait()


def in_hbm(*arrays):
    return tuple(pltpu.with_memory_space_constraint(x, pltpu.HBM) for x in arrays)


def fine_translate(pattern, inner, outer, table, partner, offset, count):
    return pl.pallas_call(
        fine_kernel,
        out_shape=jax.ShapeDtypeStruct((2, 24, 8, 128), jnp.float32),
        in_specs=[spec(pl.ANY)] * 7,
        out_specs=spec(pl.ANY),
        scratch_shapes=[
            pltpu.VMEM((2, 576, 128), jnp.float32),
            pltpu.VMEM((2, 136, 128), jnp.float32),
            pltpu.VMEM((2, 24, 8, 128), jnp.float32),
            pltpu.SMEM((16, 24), jnp.int32),
            pltpu.SMEM((16, 24), jnp.int32),
            pltpu.SMEM((24,), jnp.int32),
            pltpu.SemaphoreType.DMA((7,)),
            pltpu.SemaphoreType.DMA((3,)),
        ],
        compiler_params=PARAMS,
        cost_estimate=pl.CostEstimate(flops=4_000_000, bytes_accessed=4_000_000, transcendentals=0),
    )(*in_hbm(partner.T, offset.T, count, table.reshape(2, 128, 128)), pattern, inner, outer)


def coarse_box(b, partner_ref, offset_ref, count_ref):
    base = (lax.axis_index("box") // 2 - 2) * 6
    return [(j < count_ref[b], partner_ref[b, j] - base, offset_ref[b, j]) for j in range(16)]


def coarse_sums(window, table, slots):
    sums = [None, None]
    for live, place, which in slots:
        place = pl.multiple_of(jnp.where(live, place, 0) * 32, 32)
        scale = jnp.where(live, 1.0, 0.0)
        for half in range(2):
            lanes = slice(128 * half, 128 * half + 128)
            rows = pl.ds(place + 16 * half, 16)
            a, c = table[0, which, :, lanes] * scale, table[1, which, :, lanes] * scale
            f, g = window[0, rows], window[1, rows]
            terms = (a * f, c * g, a * g, c * f)
            old = sums[half]
            sums[half] = terms if old is None else tuple(s + t for s, t in zip(old, terms))
    return [(s[0] - s[1], s[2] + s[3]) for s in sums]


def first_kernel(partner_ref, offset_ref, count_ref, table, pair_ref, out_ref, dense_ref):
    odd = lax.rem(lax.axis_index("box"), 2) == 1
    dense_ref[...] = jnp.zeros(dense_ref.shape, jnp.float32)

    def step(b, carry):
        slots = []
        for live, box, which in coarse_box(b, partner_ref, offset_ref, count_ref):
            far = jnp.logical_and(live, jnp.where(odd, box < 12, box >= 18))
            place = jnp.where(odd, jnp.where(box >= 6, box - 6, box + 6), box - 18)
            row = pl.multiple_of(jnp.where(far, b * 12 + place, 36) * 16, 16)
            for x in range(2):
                dense_ref[x, pl.ds(row, 16)] = table[x, which]
            slots.append((live & (box >= 12) & (box < 18), box - 12, which))
        sums = coarse_sums(pair_ref, table, slots)
        for half in range(2):
            for x in range(2):
                out_ref[x, b, :, 128 * half : 128 * half + 128] = sums[half][x]
        return carry

    lax.fori_loop(0, 3, step, 0)


def second_kernel(partner_ref, offset_ref, count_ref, table, sides_ref, part_ref, out_ref):
    odd = lax.rem(lax.axis_index("box"), 2) == 1

    def step(b, carry):
        slots = []
        for live, box, which in coarse_box(b, partner_ref, offset_ref, count_ref):
            place = jnp.where(odd, box - 18, jnp.where(box >= 6, box - 6, box + 6))
            slots.append((jnp.logical_and(live, jnp.where(odd, box >= 18, box < 12)), place, which))
        sums = coarse_sums(sides_ref, table, slots)
        for half in range(2):
            lanes = slice(128 * half, 128 * half + 128)
            for x in range(2):
                out_ref[x, b, :, lanes] = part_ref[x, b, :, lanes] + sums[half][x]
        return carry

    lax.fori_loop(0, 3, step, 0)


def far_kernel(other, dense, part, out, value_ref, sems):
    copies = []
    for half in range(2):
        for top in (0, 8):
            lanes, lines = pl.ds(128 * half, 128), pl.ds(top, 8)
            sums = [(part[0, b, lines, lanes], part[1, b, lines, lanes]) for b in range(3)]
            for s in range(12):
                rows = pl.ds(32 * s + 16 * half + top, 8)
                f, g = other[0, rows], other[1, rows]
                for b in range(3):
                    places = pl.ds((12 * b + s) * 16 + top, 8)
                    a, c = dense[0, places, lanes], dense[1, places, lanes]
                    sums[b] = (sums[b][0] + (a * f - c * g), sums[b][1] + (a * g + c * f))
            for b in range(3):
                for x in range(2):
                    value_ref[x, b, lines, lanes] = sums[b][x]
            copies.append(
                pltpu.make_async_copy(
                    value_ref.at[:, :, lines, lanes], out.at[:, :, lines, lanes], sems.at[len(copies)]
                )
            )
            copies[-1].start()
    for copy in copies:
        copy.wait()


def first_translate(lists, table, pair):
    return pl.pallas_call(
        first_kernel,
        out_shape=(
            jax.ShapeDtypeStruct((2, 3, 16, 256), jnp.float32),
            jax.ShapeDtypeStruct((2, 37 * 16, 256), jnp.float32),
        ),
        in_specs=[spec(SMEM)] * 3 + [spec(VMEM)] * 2,
        out_specs=(spec(VMEM), spec(VMEM)),
        compiler_params=PARAMS,
    )(*lists, table, pair)


def second_translate(lists, table, sides, part):
    return pl.pallas_call(
        second_kernel,
        out_shape=jax.ShapeDtypeStruct((2, 3, 16, 256), jnp.float32),
        in_specs=[spec(SMEM)] * 3 + [spec(VMEM)] * 3,
        out_specs=spec(VMEM),
        compiler_params=PARAMS,
    )(*lists, table, sides, part)


def far_translate(other, dense, part):
    return pl.pallas_call(
        far_kernel,
        out_shape=jax.ShapeDtypeStruct((2, 3, 16, 256), jnp.float32),
        in_specs=[spec(VMEM)] * 3,
        out_specs=spec(pl.ANY),
        scratch_shapes=[pltpu.VMEM((2, 3, 16, 256), jnp.float32), pltpu.SemaphoreType.DMA((4,))],
        compiler_params=PARAMS,
    )(other, dense, part)


def shards(
    fine_pattern,
    fine_partner,
    fine_offset,
    fine_count,
    coarse_partner,
    coarse_offset,
    coarse_count,
    fine_table,
    coarse_table,
    theta_start,
    theta_weight,
    phi_interp,
    shift_phase,
):
    pattern = fine_pattern.reshape(2, 192, 128)
    inner = swap_cores(pattern)
    own, theta, theta_rim, phi, phi_low, cosine, sine = prepare(
        pattern, theta_start, theta_weight, phi_interp, shift_phase.reshape(128, 256)
    )
    inner, own, theta = lax.optimization_barrier((inner, own, theta))
    even, odd = rims(own, inner)
    even, odd, late = lax.optimization_barrier((even, odd, own))
    outer = swap_chips(late, 1, 1)
    even, odd = swap_rims(even, 0), swap_rims(odd, 1)
    part, *waves = aggregate(own, inner, even, theta, phi, phi_low, cosine, sine)
    pair = rim_sums(part, odd, theta_rim, phi, phi_low, *waves)
    next_to, distant = swap_chips(pair, 1, 1), swap_chips(pair, 1, 2)
    fine_incoming = fine_translate(
        own, inner, outer, fine_table, fine_partner, fine_offset, fine_count
    )
    lists = (coarse_partner, coarse_offset, coarse_count)
    part, dense = first_translate(lists, coarse_table, pair)
    distant, fine_incoming, part, dense = lax.optimization_barrier((distant, fine_incoming, part, dense))
    next_to, distant = lax.optimization_barrier((next_to, distant))
    sides = jnp.concatenate([next_to, distant], axis=1)
    other = swap_cores(sides)
    part = second_translate(lists, coarse_table, sides, part)
    coarse_incoming = far_translate(other, dense, part)
    return (fine_incoming, coarse_incoming)


def solution(mesh):
    return jax.shard_map(
        shards,
        mesh=mesh,
        in_specs=(
            P(None, "box", "samp", None),
            P("box", None),
            P("box", None),
            P("box"),
            P("box", None),
            P("box", None),
            P("box"),
            P(None, None, "samp", None),
            P(None, None, "samp", None),
            P("samp"),
            P("samp", None),
            P(),
            P(None, "samp", None),
        ),
        out_specs=(P(None, "box", "samp", None), P(None, "box", "samp", None)),
        check_vma=False,
    )
```

```python
import functools

import jax
import jax.numpy as jnp
from jax import lax
from jax.experimental import pallas as pl
from jax.experimental.pallas import tpu as pltpu
from jax.sharding import PartitionSpec as P

VMEM = pltpu.VMEM
SMEM = pltpu.SMEM
PARAMS = pltpu.CompilerParams(vmem_limit_bytes=16 * 1024 * 1024)


def spec(space):
    return pl.BlockSpec(memory_space=space)


def matched(x, axis, pairs):
    return lax.ppermute(x, axis, pairs + [(j, i) for i, j in pairs])


def swap_cores(x):
    n = lax.axis_size("box")
    return matched(x, "box", [(i, i + 1) for i in range(0, n, 2)])


def swap_chips(x, core, distance):
    n = lax.axis_size("box")
    pairs = [(i + core, i + 2 * distance + 1 - core) for i in range(0, n - 2 * distance, 2)]
    return matched(x, "box", pairs)


def swap_rims(x, start):
    n = lax.axis_size("samp")
    return matched(x, "samp", [(i, i + 1) for i in range(start, n - 1, 2)])


def rim_kernel(own_ref, inner_ref, even_ref, odd_ref):
    odd = lax.rem(lax.axis_index("samp"), 2) == 1
    for x in range(2):
        for row in range(2):
            for which, ref in enumerate((own_ref, inner_ref)):
                first = ref[x, pl.ds(row, 24, stride=8), :]
                last = ref[x, pl.ds(6 + row, 24, stride=8), :]
                boxes = pl.ds(24 * which, 24)
                even_ref[x, row, boxes] = jnp.where(odd, first, last)
                odd_ref[x, row, boxes] = jnp.where(odd, last, first)


def rims(own, inner):
    shape = jax.ShapeDtypeStruct((2, 2, 48, 128), jnp.float32)
    return pl.pallas_call(
        rim_kernel,
        out_shape=(shape, shape),
        in_specs=[spec(VMEM)] * 2,
        out_specs=(spec(VMEM), spec(VMEM)),
        compiler_params=PARAMS,
    )(own, inner)


def split(x):
    high = x.astype(jnp.bfloat16)
    return high, (x - high.astype(jnp.float32)).astype(jnp.bfloat16)


def dot(x, y):
    return jnp.dot(x, y, preferred_element_type=jnp.float32)


SINE = (-1 / 6, 1 / 120, -1 / 5040, 1 / 362880, -1 / 39916800, 1 / 6227020800)
COSINE = (-1 / 2, 1 / 24, -1 / 720, 1 / 40320, -1 / 3628800, 1 / 479001600)


def series(square, terms):
    total = square * terms[-1]
    for term in terms[-2::-1]:
        total = square * (total + term)
    return total + 1.0


def prepare_kernel(
    start,
    weight,
    pattern,
    phi,
    phase,
    own_ref,
    theta_ref,
    theta_low_ref,
    phi_out_ref,
    phi_low_ref,
    cos_ref,
    sin_ref,
    phi_ref,
    start_ref,
    weight_ref,
    sems,
):
    copies = [
        pltpu.make_async_copy(phi, phi_ref, sems.at[0]),
        pltpu.make_async_copy(phase, sin_ref, sems.at[1]),
        pltpu.make_async_copy(pattern, own_ref, sems.at[2]),
        pltpu.make_async_copy(start, start_ref, sems.at[3]),
        pltpu.make_async_copy(weight, weight_ref, sems.at[4]),
    ]
    for copy in copies[3:] + copies[:3]:
        copy.start()
    copies[3].wait()
    copies[4].wait()
    samp = lax.axis_index("samp")
    line = lax.broadcasted_iota(jnp.int32, (16, 96), 0)
    column = lax.broadcasted_iota(jnp.int32, (16, 96), 1)
    rim = (column - 64) // 8
    rim = jnp.where((rim < 2) == (lax.rem(samp, 2) == 1), rim % 2 - 2, rim % 2 + 8)
    row = jnp.where(column < 64, column % 8, rim) + samp * 8
    theta = jnp.zeros((16, 96), jnp.float32)
    for i in range(16):
        for q in range(4):
            theta = theta + jnp.where((row == start_ref[i] + q) & (line == i), weight_ref[q, i], 0.0)
    theta = jnp.concatenate([theta] * 8, axis=0)
    line = lax.broadcasted_iota(jnp.int32, (128, 96), 0)
    column = lax.broadcasted_iota(jnp.int32, (128, 96), 1)
    child = jnp.where(column < 64, column // 8, column % 8)
    theta = jnp.where(child == line // 16, theta, 0.0)
    high, low = split(theta)
    theta_ref[...] = jnp.concatenate([high, high], axis=1)
    theta_low_ref[...] = low
    copies[0].wait()
    high, low = split(phi_ref[...].T)
    phi_out_ref[...] = jnp.concatenate([high, high], axis=0)
    phi_low_ref[...] = low
    copies[1].wait()
    half = sin_ref[...] * 0.5
    square = half * half
    sine = half * series(square, SINE)
    cos_ref[...] = 1.0 - 2.0 * sine * sine
    sin_ref[...] = 2.0 * sine * series(square, COSINE)
    copies[2].wait()


def prepare(pattern, start, weight, phi, phase):
    half, full = jnp.bfloat16, jnp.float32
    shapes = (
        ((2, 192, 128), full),
        ((128, 192), half),
        ((128, 96), half),
        ((256, 256), half),
        ((128, 256), half),
        ((128, 256), full),
        ((128, 256), full),
    )
    return pl.pallas_call(
        prepare_kernel,
        out_shape=tuple(jax.ShapeDtypeStruct(*s) for s in shapes),
        in_specs=[spec(pl.ANY)] * 5,
        out_specs=(spec(VMEM),) * 7,
        scratch_shapes=[
            pltpu.VMEM((256, 128), jnp.float32),
            pltpu.SMEM((16,), jnp.int32),
            pltpu.SMEM((4, 16), jnp.float32),
            pltpu.SemaphoreType.DMA((5,)),
        ],
        compiler_params=PARAMS,
    )(*in_hbm(start, weight.T, pattern, phi, phase))


def aggregate_kernel(
    own_ref, inner_ref, even_ref, odd_ref, theta_ref, theta_low_ref, phi_ref, phi_low_ref, cos_ref, sin_ref, pair_ref
):
    theta, theta_low = theta_ref[...], theta_low_ref[...]
    phi, phi_low = phi_ref[...], phi_low_ref[...]
    for which, ref in enumerate((own_ref, inner_ref)):
        for k in range(3):
            columns = []
            for x in range(2):
                parts = [ref[x, 64 * k : 64 * k + 64]]
                for rim_ref in (even_ref, odd_ref):
                    parts += [rim_ref[x, r, pl.ds(24 * which + 8 * k, 8)] for r in range(2)]
                columns.append(jnp.concatenate(parts, axis=0))
            high, low = split(jnp.concatenate(columns, axis=1))
            narrow = dot(theta, jnp.concatenate([high, low], axis=0)) + dot(theta_low, high)
            high, low = split(narrow)
            wide = []
            for x in range(2):
                part = slice(128 * x, 128 * x + 128)
                both = jnp.concatenate([high[:, part], low[:, part]], axis=1)
                wide.append(dot(both, phi) + dot(high[:, part], phi_low))
            cosine, sine = cos_ref[...], sin_ref[...]
            real_part = (cosine * wide[0] - sine * wide[1]).reshape(8, 16, 256)
            imag_part = (cosine * wide[1] + sine * wide[0]).reshape(8, 16, 256)
            for x, value in enumerate((real_part, imag_part)):
                value = jnp.sum(value, axis=0)
                for half in range(2):
                    rows = pl.ds(96 * which + 32 * k + 16 * half, 16)
                    pair_ref[x, rows] = value[:, 128 * half : 128 * half + 128]


def aggregate(own, inner, even, odd, mats):
    return pl.pallas_call(
        aggregate_kernel,
        out_shape=jax.ShapeDtypeStruct((2, 192, 128), jnp.float32),
        in_specs=[spec(VMEM)] * 10,
        out_specs=spec(VMEM),
        compiler_params=PARAMS,
    )(own, inner, even, odd, *mats)


def fine_kernel(
    partner,
    offset,
    count,
    table,
    own,
    inner,
    outer,
    out,
    window,
    operators,
    value_ref,
    partner_ref,
    offset_ref,
    count_ref,
    sems,
    out_sems,
):
    me = lax.axis_index("box")
    odd = lax.rem(me, 2)
    moves = (
        (partner, partner_ref),
        (offset, offset_ref),
        (count, count_ref),
        (table, operators.at[:, pl.ds(0, 128)]),
        (own, window.at[:, pl.ds(192, 192)]),
        (inner, window.at[:, pl.ds(384 * (1 - odd), 192)]),
        (outer, window.at[:, pl.ds(384 * odd, 192)]),
    )
    copies = [pltpu.make_async_copy(*move, sems.at[i]) for i, move in enumerate(moves)]
    for copy in copies:
        copy.start()
    operators[:, 128:] = jnp.zeros((2, 8, 128), jnp.float32)
    for copy in copies:
        copy.wait()
    base = (me - 1) * 24

    def step(b, carry):
        sums = None
        for j in range(16):
            place = pl.multiple_of((partner_ref[j, b] - base) * 8, 8)
            which = pl.multiple_of(jnp.where(j < count_ref[b], offset_ref[j, b], 16) * 8, 8)
            a, c = operators[0, pl.ds(which, 8)], operators[1, pl.ds(which, 8)]
            f, g = window[0, pl.ds(place, 8)], window[1, pl.ds(place, 8)]
            terms = (a * f, c * g, a * g, c * f)
            sums = terms if sums is None else tuple(s + t for s, t in zip(sums, terms))
        value_ref[0, b] = sums[0] - sums[1]
        value_ref[1, b] = sums[2] + sums[3]
        return carry

    copies = []
    for part in range(3):
        lax.fori_loop(8 * part, 8 * part + 8, step, 0)
        boxes = pl.ds(8 * part, 8)
        copies.append(pltpu.make_async_copy(value_ref.at[:, boxes], out.at[:, boxes], out_sems.at[part]))
        copies[part].start()
    for copy in copies:
        copy.wait()


def in_hbm(*arrays):
    return tuple(pltpu.with_memory_space_constraint(x, pltpu.HBM) for x in arrays)


def fine_translate(pattern, inner, outer, table, partner, offset, count):
    return pl.pallas_call(
        fine_kernel,
        out_shape=jax.ShapeDtypeStruct((2, 24, 8, 128), jnp.float32),
        in_specs=[spec(pl.ANY)] * 7,
        out_specs=spec(pl.ANY),
        scratch_shapes=[
            pltpu.VMEM((2, 576, 128), jnp.float32),
            pltpu.VMEM((2, 136, 128), jnp.float32),
            pltpu.VMEM((2, 24, 8, 128), jnp.float32),
            pltpu.SMEM((16, 24), jnp.int32),
            pltpu.SMEM((16, 24), jnp.int32),
            pltpu.SMEM((24,), jnp.int32),
            pltpu.SemaphoreType.DMA((7,)),
            pltpu.SemaphoreType.DMA((3,)),
        ],
        compiler_params=PARAMS,
        cost_estimate=pl.CostEstimate(flops=4_000_000, bytes_accessed=4_000_000, transcendentals=0),
    )(*in_hbm(partner.T, offset.T, count, table.reshape(2, 128, 128)), pattern, inner, outer)


SIDE, SOURCES = 12, 21


def first_kernel(partner_ref, offset_ref, count_ref, table, pair_ref, out_ref, dense_ref):
    me = lax.axis_index("box")
    odd = lax.rem(me, 2) == 1
    base = (me // 2 - 2) * 6
    firsts = [jnp.where(odd, *of) for of in ((18, 6), (12, 0), (0, 12), (6, 18))]
    turned = jnp.where(odd, 18, 12)
    dense_ref[...] = jnp.zeros(dense_ref.shape, jnp.float32)

    def pick(box, values):
        before = jnp.where(box < 6, values[0], values[1])
        return jnp.where(box < 12, before, jnp.where(box < 24, values[2], values[3]))

    def step(b, carry):
        sums = [None, None]
        for j in range(16):
            live = j < count_ref[b]
            box, which = partner_ref[b, j] - base, offset_ref[b, j]
            here = jnp.logical_and(box >= 12, box < 18)
            place = box - jnp.where(here, 12, pick(box, (0, 6, 18, 24)))
            place = jnp.where(box < turned, jnp.where(place < 3, place + 3, place - 3), place)
            away = jnp.logical_and(live, jnp.logical_not(here))
            entry = jnp.where(away, b * SOURCES + pick(box, firsts) + place, 3 * SOURCES)
            row = pl.multiple_of(entry * 16, 16)
            for x in range(2):
                dense_ref[x, pl.ds(row, 16)] = table[x, which]
            here = jnp.logical_and(live, here)
            place = pl.multiple_of(jnp.where(here, place, 0) * 32, 32)
            scale = jnp.where(here, 1.0, 0.0)
            for half in range(2):
                lanes = slice(128 * half, 128 * half + 128)
                rows = pl.ds(place + 16 * half, 16)
                a, c = table[0, which, :, lanes] * scale, table[1, which, :, lanes] * scale
                f, g = pair_ref[0, rows], pair_ref[1, rows]
                terms = (a * f, c * g, a * g, c * f)
                old = sums[half]
                sums[half] = terms if old is None else tuple(s + t for s, t in zip(old, terms))
        for half in range(2):
            lanes = slice(128 * half, 128 * half + 128)
            out_ref[0, b, :, lanes] = sums[half][0] - sums[half][1]
            out_ref[1, b, :, lanes] = sums[half][2] + sums[half][3]
        return carry

    lax.fori_loop(0, 3, step, 0)


def dense_sums(part, dense, sources, lines, lanes, half, top):
    sums = [(part[0, b, lines, lanes], part[1, b, lines, lanes]) for b in range(3)]
    for ref, row, entry in sources:
        rows = pl.ds(row + 16 * half + top, 8)
        f, g = ref[0, rows], ref[1, rows]
        for b in range(3):
            places = pl.ds((SOURCES * b + entry) * 16 + top, 8)
            a, c = dense[0, places, lanes], dense[1, places, lanes]
            sums[b] = (sums[b][0] + (a * f - c * g), sums[b][1] + (a * g + c * f))
    return sums


def second_kernel(next_ref, distant_ref, dense, part, out_ref):
    sources = [(next_ref, 32 * s, s) for s in range(6)] + [(distant_ref, 32 * s, 6 + s) for s in range(6)]
    for half in range(2):
        for top in (0, 8):
            lanes, lines = pl.ds(128 * half, 128), pl.ds(top, 8)
            sums = dense_sums(part, dense, sources, lines, lanes, half, top)
            for b in range(3):
                for x in range(2):
                    out_ref[x, b, lines, lanes] = sums[b][x]


def far_kernel(other, dense, part, out, value_ref, sems):
    sources = [(other, 32 * s, SIDE + s) for s in range(9)]
    copies = []
    for half in range(2):
        for top in (0, 8):
            lanes, lines = pl.ds(128 * half, 128), pl.ds(top, 8)
            sums = dense_sums(part, dense, sources, lines, lanes, half, top)
            for b in range(3):
                for x in range(2):
                    value_ref[x, b, lines, lanes] = sums[b][x]
            copies.append(
                pltpu.make_async_copy(
                    value_ref.at[:, :, lines, lanes], out.at[:, :, lines, lanes], sems.at[len(copies)]
                )
            )
            copies[-1].start()
    for copy in copies:
        copy.wait()


def first_translate(lists, table, pair):
    return pl.pallas_call(
        first_kernel,
        out_shape=(
            jax.ShapeDtypeStruct((2, 3, 16, 256), jnp.float32),
            jax.ShapeDtypeStruct((2, (3 * SOURCES + 1) * 16, 256), jnp.float32),
        ),
        in_specs=[spec(SMEM)] * 3 + [spec(VMEM)] * 2,
        out_specs=(spec(VMEM), spec(VMEM)),
        compiler_params=PARAMS,
    )(*lists, table, pair)


def second_translate(next_to, distant, dense, part):
    return pl.pallas_call(
        second_kernel,
        out_shape=jax.ShapeDtypeStruct((2, 3, 16, 256), jnp.float32),
        in_specs=[spec(VMEM)] * 4,
        out_specs=spec(VMEM),
        compiler_params=PARAMS,
    )(next_to, distant, dense, part)


def far_translate(other, dense, part):
    return pl.pallas_call(
        far_kernel,
        out_shape=jax.ShapeDtypeStruct((2, 3, 16, 256), jnp.float32),
        in_specs=[spec(VMEM)] * 3,
        out_specs=spec(pl.ANY),
        scratch_shapes=[pltpu.VMEM((2, 3, 16, 256), jnp.float32), pltpu.SemaphoreType.DMA((4,))],
        compiler_params=PARAMS,
    )(other, dense, part)


def shards(
    fine_pattern,
    fine_partner,
    fine_offset,
    fine_count,
    coarse_partner,
    coarse_offset,
    coarse_count,
    fine_table,
    coarse_table,
    theta_start,
    theta_weight,
    phi_interp,
    shift_phase,
):
    pattern = fine_pattern.reshape(2, 192, 128)
    inner = swap_cores(pattern)
    own, *mats = prepare(pattern, theta_start, theta_weight, phi_interp, shift_phase.reshape(128, 256))
    inner, own, mats = lax.optimization_barrier((inner, own, mats))
    even, odd = rims(own, inner)
    even, odd, late = lax.optimization_barrier((even, odd, own))
    outer = swap_chips(late, 1, 1)
    even, odd = swap_rims(even, 0), swap_rims(odd, 1)
    pair = aggregate(own, inner, even, odd, mats)
    next_to, distant = swap_chips(pair, 1, 1), swap_chips(pair, 1, 2)
    fine_incoming = fine_translate(
        own, inner, outer, fine_table, fine_partner, fine_offset, fine_count
    )
    lists = (coarse_partner, coarse_offset, coarse_count)
    part, dense = first_translate(lists, coarse_table, pair)
    distant, fine_incoming, part, dense = lax.optimization_barrier((distant, fine_incoming, part, dense))
    next_to, distant = lax.optimization_barrier((next_to, distant))
    other = swap_cores(jnp.concatenate([next_to, distant[:, :96]], axis=1))
    part = second_translate(next_to, distant, dense, part)
    coarse_incoming = far_translate(other, dense, part)
    return (fine_incoming, coarse_incoming)


def solution(mesh):
    return jax.shard_map(
        shards,
        mesh=mesh,
        in_specs=(
            P(None, "box", "samp", None),
            P("box", None),
            P("box", None),
            P("box"),
            P("box", None),
            P("box", None),
            P("box"),
            P(None, None, "samp", None),
            P(None, None, "samp", None),
            P("samp"),
            P("samp", None),
            P(),
            P(None, "samp", None),
        ),
        out_specs=(P(None, "box", "samp", None), P(None, "box", "samp", None)),
        check_vma=False,
    )
```

```python
import functools

import jax
import jax.numpy as jnp
from jax import lax
from jax.experimental import pallas as pl
from jax.experimental.pallas import tpu as pltpu
from jax.sharding import PartitionSpec as P

VMEM = pltpu.VMEM
SMEM = pltpu.SMEM
PARAMS = pltpu.CompilerParams(vmem_limit_bytes=16 * 1024 * 1024)


def spec(space):
    return pl.BlockSpec(memory_space=space)


def matched(x, axis, pairs):
    return lax.ppermute(x, axis, pairs + [(j, i) for i, j in pairs])


def swap_cores(x):
    n = lax.axis_size("box")
    return matched(x, "box", [(i, i + 1) for i in range(0, n, 2)])


def swap_chips(x, core, distance):
    n = lax.axis_size("box")
    pairs = [(i + core, i + 2 * distance + 1 - core) for i in range(0, n - 2 * distance, 2)]
    return matched(x, "box", pairs)


def swap_rims(x, start):
    n = lax.axis_size("samp")
    return matched(x, "samp", [(i, i + 1) for i in range(start, n - 1, 2)])


def rim_kernel(own_ref, inner_ref, even_ref, odd_ref):
    odd = lax.rem(lax.axis_index("samp"), 2) == 1
    for x in range(2):
        for row in range(2):
            for which, ref in enumerate((own_ref, inner_ref)):
                first = ref[x, pl.ds(row, 24, stride=8), :]
                last = ref[x, pl.ds(6 + row, 24, stride=8), :]
                boxes = pl.ds(24 * which, 24)
                even_ref[x, row, boxes] = jnp.where(odd, first, last)
                odd_ref[x, row, boxes] = jnp.where(odd, last, first)


def rims(own, inner):
    shape = jax.ShapeDtypeStruct((2, 2, 48, 128), jnp.float32)
    return pl.pallas_call(
        rim_kernel,
        out_shape=(shape, shape),
        in_specs=[spec(VMEM)] * 2,
        out_specs=(spec(VMEM), spec(VMEM)),
        compiler_params=PARAMS,
    )(own, inner)


def split(x):
    high = x.astype(jnp.bfloat16)
    return high, (x - high.astype(jnp.float32)).astype(jnp.bfloat16)


def dot(x, y):
    return jnp.dot(x, y, preferred_element_type=jnp.float32)


SINE = (-1 / 6, 1 / 120, -1 / 5040, 1 / 362880, -1 / 39916800, 1 / 6227020800)
COSINE = (-1 / 2, 1 / 24, -1 / 720, 1 / 40320, -1 / 3628800, 1 / 479001600)


def series(square, terms):
    total = square * terms[-1]
    for term in terms[-2::-1]:
        total = square * (total + term)
    return total + 1.0


def prepare_kernel(
    start,
    weight,
    pattern,
    phi,
    phase,
    own_ref,
    theta_ref,
    theta_low_ref,
    phi_out_ref,
    phi_low_ref,
    cos_ref,
    sin_ref,
    phi_ref,
    start_ref,
    weight_ref,
    sems,
):
    copies = [
        pltpu.make_async_copy(phi, phi_ref, sems.at[0]),
        pltpu.make_async_copy(phase, sin_ref, sems.at[1]),
        pltpu.make_async_copy(pattern, own_ref, sems.at[2]),
        pltpu.make_async_copy(start, start_ref, sems.at[3]),
        pltpu.make_async_copy(weight, weight_ref, sems.at[4]),
    ]
    for copy in copies[3:] + copies[:3]:
        copy.start()
    copies[3].wait()
    copies[4].wait()
    samp = lax.axis_index("samp")
    line = lax.broadcasted_iota(jnp.int32, (16, 96), 0)
    column = lax.broadcasted_iota(jnp.int32, (16, 96), 1)
    rim = (column - 64) // 8
    rim = jnp.where((rim < 2) == (lax.rem(samp, 2) == 1), rim % 2 - 2, rim % 2 + 8)
    row = jnp.where(column < 64, column % 8, rim) + samp * 8
    theta = jnp.zeros((16, 96), jnp.float32)
    for i in range(16):
        for q in range(4):
            theta = theta + jnp.where((row == start_ref[i] + q) & (line == i), weight_ref[q, i], 0.0)
    theta = jnp.concatenate([theta] * 8, axis=0)
    line = lax.broadcasted_iota(jnp.int32, (128, 96), 0)
    column = lax.broadcasted_iota(jnp.int32, (128, 96), 1)
    child = jnp.where(column < 64, column // 8, column % 8)
    theta = jnp.where(child == line // 16, theta, 0.0)
    high, low = split(theta)
    theta_ref[...] = jnp.concatenate([high, high], axis=1)
    theta_low_ref[...] = low
    copies[0].wait()
    high, low = split(phi_ref[...].T)
    phi_out_ref[...] = jnp.concatenate([high, high], axis=0)
    phi_low_ref[...] = low
    copies[1].wait()
    half = sin_ref[...] * 0.5
    square = half * half
    sine = half * series(square, SINE)
    cos_ref[...] = 1.0 - 2.0 * sine * sine
    sin_ref[...] = 2.0 * sine * series(square, COSINE)
    copies[2].wait()


def prepare(pattern, start, weight, phi, phase):
    half, full = jnp.bfloat16, jnp.float32
    shapes = (
        ((2, 192, 128), full),
        ((128, 192), half),
        ((128, 96), half),
        ((256, 256), half),
        ((128, 256), half),
        ((128, 256), full),
        ((128, 256), full),
    )
    return pl.pallas_call(
        prepare_kernel,
        out_shape=tuple(jax.ShapeDtypeStruct(*s) for s in shapes),
        in_specs=[spec(pl.ANY)] * 5,
        out_specs=(spec(VMEM),) * 7,
        scratch_shapes=[
            pltpu.VMEM((256, 128), jnp.float32),
            pltpu.SMEM((16,), jnp.int32),
            pltpu.SMEM((4, 16), jnp.float32),
            pltpu.SemaphoreType.DMA((5,)),
        ],
        compiler_params=PARAMS,
    )(*in_hbm(start, weight.T, pattern, phi, phase))


def aggregate_kernel(
    own_ref, inner_ref, even_ref, odd_ref, theta_ref, theta_low_ref, phi_ref, phi_low_ref, cos_ref, sin_ref, pair_ref
):
    theta, theta_low = theta_ref[...], theta_low_ref[...]
    phi, phi_low = phi_ref[...], phi_low_ref[...]

    def narrow_of(box):
        ref, k = (own_ref, inner_ref)[box // 3], box % 3
        columns = []
        for x in range(2):
            parts = [ref[x, 64 * k : 64 * k + 64]]
            for rim_ref in (even_ref, odd_ref):
                parts += [rim_ref[x, r, pl.ds(8 * box, 8)] for r in range(2)]
            columns.append(jnp.concatenate(parts, axis=0))
        high, low = split(jnp.concatenate(columns, axis=1))
        return dot(theta, jnp.concatenate([high, low], axis=0)) + dot(theta_low, high)

    def wide_of(narrow):
        high, low = split(narrow)
        wide = []
        for x in range(2):
            part = slice(128 * x, 128 * x + 128)
            both = jnp.concatenate([high[:, part], low[:, part]], axis=1)
            wide.append(dot(both, phi) + dot(high[:, part], phi_low))
        return wide

    def store(box, wide):
        cosine, sine = cos_ref[...], sin_ref[...]
        real_part = (cosine * wide[0] - sine * wide[1]).reshape(8, 16, 256)
        imag_part = (cosine * wide[1] + sine * wide[0]).reshape(8, 16, 256)
        for x, value in enumerate((real_part, imag_part)):
            value = jnp.sum(value, axis=0)
            for half in range(2):
                rows = pl.ds(32 * box + 16 * half, 16)
                pair_ref[x, rows] = value[:, 128 * half : 128 * half + 128]

    narrow = [narrow_of(0), narrow_of(1)]
    wide = wide_of(narrow[0])
    for box in range(6):
        if box < 4:
            narrow.append(narrow_of(box + 2))
        ahead = wide_of(narrow[box + 1]) if box < 5 else None
        store(box, wide)
        wide = ahead


def aggregate(own, inner, even, odd, mats):
    return pl.pallas_call(
        aggregate_kernel,
        out_shape=jax.ShapeDtypeStruct((2, 192, 128), jnp.float32),
        in_specs=[spec(VMEM)] * 10,
        out_specs=spec(VMEM),
        compiler_params=PARAMS,
    )(own, inner, even, odd, *mats)


def fine_kernel(
    partner,
    offset,
    count,
    table,
    own,
    inner,
    outer,
    out,
    window,
    operators,
    value_ref,
    partner_ref,
    offset_ref,
    count_ref,
    sems,
    out_sems,
):
    me = lax.axis_index("box")
    odd = lax.rem(me, 2)
    moves = (
        (partner, partner_ref),
        (offset, offset_ref),
        (count, count_ref),
        (table, operators.at[:, pl.ds(0, 128)]),
        (own, window.at[:, pl.ds(192, 192)]),
        (inner, window.at[:, pl.ds(384 * (1 - odd), 192)]),
        (outer, window.at[:, pl.ds(384 * odd, 192)]),
    )
    copies = [pltpu.make_async_copy(*move, sems.at[i]) for i, move in enumerate(moves)]
    for copy in copies:
        copy.start()
    operators[:, 128:] = jnp.zeros((2, 8, 128), jnp.float32)
    for copy in copies:
        copy.wait()
    base = (me - 1) * 24

    def step(b, carry):
        sums = None
        for j in range(16):
            place = pl.multiple_of((partner_ref[j, b] - base) * 8, 8)
            which = pl.multiple_of(jnp.where(j < count_ref[b], offset_ref[j, b], 16) * 8, 8)
            a, c = operators[0, pl.ds(which, 8)], operators[1, pl.ds(which, 8)]
            f, g = window[0, pl.ds(place, 8)], window[1, pl.ds(place, 8)]
            terms = (a * f, c * g, a * g, c * f)
            sums = terms if sums is None else tuple(s + t for s, t in zip(sums, terms))
        value_ref[0, b] = sums[0] - sums[1]
        value_ref[1, b] = sums[2] + sums[3]
        return carry

    copies = []
    for part in range(3):
        lax.fori_loop(8 * part, 8 * part + 8, step, 0)
        boxes = pl.ds(8 * part, 8)
        copies.append(pltpu.make_async_copy(value_ref.at[:, boxes], out.at[:, boxes], out_sems.at[part]))
        copies[part].start()
    for copy in copies:
        copy.wait()


def in_hbm(*arrays):
    return tuple(pltpu.with_memory_space_constraint(x, pltpu.HBM) for x in arrays)


def fine_translate(pattern, inner, outer, table, partner, offset, count):
    return pl.pallas_call(
        fine_kernel,
        out_shape=jax.ShapeDtypeStruct((2, 24, 8, 128), jnp.float32),
        in_specs=[spec(pl.ANY)] * 7,
        out_specs=spec(pl.ANY),
        scratch_shapes=[
            pltpu.VMEM((2, 576, 128), jnp.float32),
            pltpu.VMEM((2, 136, 128), jnp.float32),
            pltpu.VMEM((2, 24, 8, 128), jnp.float32),
            pltpu.SMEM((16, 24), jnp.int32),
            pltpu.SMEM((16, 24), jnp.int32),
            pltpu.SMEM((24,), jnp.int32),
            pltpu.SemaphoreType.DMA((7,)),
            pltpu.SemaphoreType.DMA((3,)),
        ],
        compiler_params=PARAMS,
        cost_estimate=pl.CostEstimate(flops=4_000_000, bytes_accessed=4_000_000, transcendentals=0),
    )(*in_hbm(partner.T, offset.T, count, table.reshape(2, 128, 128)), pattern, inner, outer)


SIDE, SOURCES = 12, 21


def first_kernel(partner_ref, offset_ref, count_ref, table, pair_ref, out_ref, dense_ref):
    me = lax.axis_index("box")
    odd = lax.rem(me, 2) == 1
    base = (me // 2 - 2) * 6
    firsts = [jnp.where(odd, *of) for of in ((18, 6), (12, 0), (0, 12), (6, 18))]
    turned = jnp.where(odd, 18, 12)
    dense_ref[...] = jnp.zeros(dense_ref.shape, jnp.float32)

    def pick(box, values):
        before = jnp.where(box < 6, values[0], values[1])
        return jnp.where(box < 12, before, jnp.where(box < 24, values[2], values[3]))

    def step(b, carry):
        sums = [None, None]
        for j in range(16):
            live = j < count_ref[b]
            box, which = partner_ref[b, j] - base, offset_ref[b, j]
            here = jnp.logical_and(box >= 12, box < 18)
            place = box - jnp.where(here, 12, pick(box, (0, 6, 18, 24)))
            place = jnp.where(box < turned, jnp.where(place < 3, place + 3, place - 3), place)
            away = jnp.logical_and(live, jnp.logical_not(here))
            entry = jnp.where(away, b * SOURCES + pick(box, firsts) + place, 3 * SOURCES)
            row = pl.multiple_of(entry * 16, 16)
            for x in range(2):
                dense_ref[x, pl.ds(row, 16)] = table[x, which]
            here = jnp.logical_and(live, here)
            place = pl.multiple_of(jnp.where(here, place, 0) * 32, 32)
            scale = jnp.where(here, 1.0, 0.0)
            for half in range(2):
                lanes = slice(128 * half, 128 * half + 128)
                rows = pl.ds(place + 16 * half, 16)
                a, c = table[0, which, :, lanes] * scale, table[1, which, :, lanes] * scale
                f, g = pair_ref[0, rows], pair_ref[1, rows]
                terms = (a * f, c * g, a * g, c * f)
                old = sums[half]
                sums[half] = terms if old is None else tuple(s + t for s, t in zip(old, terms))
        for half in range(2):
            lanes = slice(128 * half, 128 * half + 128)
            out_ref[0, b, :, lanes] = sums[half][0] - sums[half][1]
            out_ref[1, b, :, lanes] = sums[half][2] + sums[half][3]
        return carry

    lax.fori_loop(0, 3, step, 0)


def dense_sums(part, dense, sources, lines, lanes, half, top):
    sums = [(part[0, b, lines, lanes], part[1, b, lines, lanes]) for b in range(3)]
    for ref, row, entry in sources:
        rows = pl.ds(row + 16 * half + top, 8)
        f, g = ref[0, rows], ref[1, rows]
        for b in range(3):
            places = pl.ds((SOURCES * b + entry) * 16 + top, 8)
            a, c = dense[0, places, lanes], dense[1, places, lanes]
            sums[b] = (sums[b][0] + (a * f - c * g), sums[b][1] + (a * g + c * f))
    return sums


def second_kernel(next_ref, distant_ref, dense, part, out_ref):
    sources = [(next_ref, 32 * s, s) for s in range(6)] + [(distant_ref, 32 * s, 6 + s) for s in range(6)]
    for half in range(2):
        for top in (0, 8):
            lanes, lines = pl.ds(128 * half, 128), pl.ds(top, 8)
            sums = dense_sums(part, dense, sources, lines, lanes, half, top)
            for b in range(3):
                for x in range(2):
                    out_ref[x, b, lines, lanes] = sums[b][x]


def far_kernel(other, dense, part, out, value_ref, sems):
    sources = [(other, 32 * s, SIDE + s) for s in range(9)]
    copies = []
    for half in range(2):
        for top in (0, 8):
            lanes, lines = pl.ds(128 * half, 128), pl.ds(top, 8)
            sums = dense_sums(part, dense, sources, lines, lanes, half, top)
            for b in range(3):
                for x in range(2):
                    value_ref[x, b, lines, lanes] = sums[b][x]
            copies.append(
                pltpu.make_async_copy(
                    value_ref.at[:, :, lines, lanes], out.at[:, :, lines, lanes], sems.at[len(copies)]
                )
            )
            copies[-1].start()
    for copy in copies:
        copy.wait()


def first_translate(lists, table, pair):
    return pl.pallas_call(
        first_kernel,
        out_shape=(
            jax.ShapeDtypeStruct((2, 3, 16, 256), jnp.float32),
            jax.ShapeDtypeStruct((2, (3 * SOURCES + 1) * 16, 256), jnp.float32),
        ),
        in_specs=[spec(SMEM)] * 3 + [spec(VMEM)] * 2,
        out_specs=(spec(VMEM), spec(VMEM)),
        compiler_params=PARAMS,
    )(*lists, table, pair)


def second_translate(next_to, distant, dense, part):
    return pl.pallas_call(
        second_kernel,
        out_shape=jax.ShapeDtypeStruct((2, 3, 16, 256), jnp.float32),
        in_specs=[spec(VMEM)] * 4,
        out_specs=spec(VMEM),
        compiler_params=PARAMS,
    )(next_to, distant, dense, part)


def far_translate(other, dense, part):
    return pl.pallas_call(
        far_kernel,
        out_shape=jax.ShapeDtypeStruct((2, 3, 16, 256), jnp.float32),
        in_specs=[spec(VMEM)] * 3,
        out_specs=spec(pl.ANY),
        scratch_shapes=[pltpu.VMEM((2, 3, 16, 256), jnp.float32), pltpu.SemaphoreType.DMA((4,))],
        compiler_params=PARAMS,
    )(other, dense, part)


def shards(
    fine_pattern,
    fine_partner,
    fine_offset,
    fine_count,
    coarse_partner,
    coarse_offset,
    coarse_count,
    fine_table,
    coarse_table,
    theta_start,
    theta_weight,
    phi_interp,
    shift_phase,
):
    pattern = fine_pattern.reshape(2, 192, 128)
    inner = swap_cores(pattern)
    own, *mats = prepare(pattern, theta_start, theta_weight, phi_interp, shift_phase.reshape(128, 256))
    inner, own, mats = lax.optimization_barrier((inner, own, mats))
    even, odd = rims(own, inner)
    even, odd, late = lax.optimization_barrier((even, odd, own))
    outer = swap_chips(late, 1, 1)
    even, odd = swap_rims(even, 0), swap_rims(odd, 1)
    pair = aggregate(own, inner, even, odd, mats)
    next_to, distant = swap_chips(pair, 1, 1), swap_chips(pair, 1, 2)
    fine_incoming = fine_translate(
        own, inner, outer, fine_table, fine_partner, fine_offset, fine_count
    )
    lists = (coarse_partner, coarse_offset, coarse_count)
    part, dense = first_translate(lists, coarse_table, pair)
    distant, fine_incoming, part, dense = lax.optimization_barrier((distant, fine_incoming, part, dense))
    next_to, distant = lax.optimization_barrier((next_to, distant))
    other = swap_cores(jnp.concatenate([next_to, distant[:, :96]], axis=1))
    part = second_translate(next_to, distant, dense, part)
    coarse_incoming = far_translate(other, dense, part)
    return (fine_incoming, coarse_incoming)


def solution(mesh):
    return jax.shard_map(
        shards,
        mesh=mesh,
        in_specs=(
            P(None, "box", "samp", None),
            P("box", None),
            P("box", None),
            P("box"),
            P("box", None),
            P("box", None),
            P("box"),
            P(None, None, "samp", None),
            P(None, None, "samp", None),
            P("samp"),
            P("samp", None),
            P(),
            P(None, "samp", None),
        ),
        out_specs=(P(None, "box", "samp", None), P(None, "box", "samp", None)),
        check_vma=False,
    )
```

```python
import functools

import jax
import jax.numpy as jnp
from jax import lax
from jax.experimental import pallas as pl
from jax.experimental.pallas import tpu as pltpu
from jax.sharding import PartitionSpec as P

VMEM = pltpu.VMEM
SMEM = pltpu.SMEM
PARAMS = pltpu.CompilerParams(vmem_limit_bytes=16 * 1024 * 1024)


def spec(space):
    return pl.BlockSpec(memory_space=space)


def matched(x, axis, pairs):
    return lax.ppermute(x, axis, pairs + [(j, i) for i, j in pairs])


def swap_cores(x):
    n = lax.axis_size("box")
    return matched(x, "box", [(i, i + 1) for i in range(0, n, 2)])


def swap_chips(x, core, distance):
    n = lax.axis_size("box")
    pairs = [(i + core, i + 2 * distance + 1 - core) for i in range(0, n - 2 * distance, 2)]
    return matched(x, "box", pairs)


def swap_next(x):
    n = lax.axis_size("box")
    return matched(x, "box", [(i, i + 2) for i in range(0, n - 2, 4)] + [(i, i + 2) for i in range(3, n - 2, 4)])


def swap_rims(x, start):
    n = lax.axis_size("samp")
    return matched(x, "samp", [(i, i + 1) for i in range(start, n - 1, 2)])


def rim_kernel(own_ref, inner_ref, even_ref, odd_ref):
    odd = lax.rem(lax.axis_index("samp"), 2) == 1
    for x in range(2):
        for row in range(2):
            for which, ref in enumerate((own_ref, inner_ref)):
                first = ref[x, pl.ds(row, 24, stride=8), :]
                last = ref[x, pl.ds(6 + row, 24, stride=8), :]
                boxes = pl.ds(24 * which, 24)
                even_ref[x, row, boxes] = jnp.where(odd, first, last)
                odd_ref[x, row, boxes] = jnp.where(odd, last, first)


def rims(own, inner):
    shape = jax.ShapeDtypeStruct((2, 2, 48, 128), jnp.float32)
    return pl.pallas_call(
        rim_kernel,
        out_shape=(shape, shape),
        in_specs=[spec(VMEM)] * 2,
        out_specs=(spec(VMEM), spec(VMEM)),
        compiler_params=PARAMS,
    )(own, inner)


def split(x):
    high = x.astype(jnp.bfloat16)
    return high, (x - high.astype(jnp.float32)).astype(jnp.bfloat16)


def dot(x, y):
    return jnp.dot(x, y, preferred_element_type=jnp.float32)


SINE = (-1 / 6, 1 / 120, -1 / 5040, 1 / 362880, -1 / 39916800, 1 / 6227020800)
COSINE = (-1 / 2, 1 / 24, -1 / 720, 1 / 40320, -1 / 3628800, 1 / 479001600)


def series(square, terms):
    total = square * terms[-1]
    for term in terms[-2::-1]:
        total = square * (total + term)
    return total + 1.0


def prepare_kernel(
    start,
    weight,
    pattern,
    phi,
    phase,
    own_ref,
    theta_ref,
    theta_low_ref,
    phi_out_ref,
    phi_low_ref,
    cos_ref,
    sin_ref,
    phi_ref,
    start_ref,
    weight_ref,
    sems,
):
    copies = [
        pltpu.make_async_copy(phi, phi_ref, sems.at[0]),
        pltpu.make_async_copy(phase, sin_ref, sems.at[1]),
        pltpu.make_async_copy(pattern, own_ref, sems.at[2]),
        pltpu.make_async_copy(start, start_ref, sems.at[3]),
        pltpu.make_async_copy(weight, weight_ref, sems.at[4]),
    ]
    for copy in copies[3:] + copies[:3]:
        copy.start()
    copies[3].wait()
    copies[4].wait()
    samp = lax.axis_index("samp")
    line = lax.broadcasted_iota(jnp.int32, (16, 96), 0)
    column = lax.broadcasted_iota(jnp.int32, (16, 96), 1)
    rim = (column - 64) // 8
    rim = jnp.where((rim < 2) == (lax.rem(samp, 2) == 1), rim % 2 - 2, rim % 2 + 8)
    row = jnp.where(column < 64, column % 8, rim) + samp * 8
    theta = jnp.zeros((16, 96), jnp.float32)
    for i in range(16):
        for q in range(4):
            theta = theta + jnp.where((row == start_ref[i] + q) & (line == i), weight_ref[q, i], 0.0)
    theta = jnp.concatenate([theta] * 8, axis=0)
    line = lax.broadcasted_iota(jnp.int32, (128, 96), 0)
    column = lax.broadcasted_iota(jnp.int32, (128, 96), 1)
    child = jnp.where(column < 64, column // 8, column % 8)
    theta = jnp.where(child == line // 16, theta, 0.0)
    high, low = split(theta)
    theta_ref[...] = jnp.concatenate([high, high], axis=1)
    theta_low_ref[...] = low
    copies[0].wait()
    high, low = split(phi_ref[...].T)
    phi_out_ref[...] = jnp.concatenate([high, high], axis=0)
    phi_low_ref[...] = low
    copies[1].wait()
    half = sin_ref[...] * 0.5
    square = half * half
    sine = half * series(square, SINE)
    cos_ref[...] = 1.0 - 2.0 * sine * sine
    sin_ref[...] = 2.0 * sine * series(square, COSINE)
    copies[2].wait()


def prepare(pattern, start, weight, phi, phase):
    half, full = jnp.bfloat16, jnp.float32
    shapes = (
        ((2, 192, 128), full),
        ((128, 192), half),
        ((128, 96), half),
        ((256, 256), half),
        ((128, 256), half),
        ((128, 256), full),
        ((128, 256), full),
    )
    return pl.pallas_call(
        prepare_kernel,
        out_shape=tuple(jax.ShapeDtypeStruct(*s) for s in shapes),
        in_specs=[spec(pl.ANY)] * 5,
        out_specs=(spec(VMEM),) * 7,
        scratch_shapes=[
            pltpu.VMEM((256, 128), jnp.float32),
            pltpu.SMEM((16,), jnp.int32),
            pltpu.SMEM((4, 16), jnp.float32),
            pltpu.SemaphoreType.DMA((5,)),
        ],
        compiler_params=PARAMS,
    )(*in_hbm(start, weight.T, pattern, phi, phase))


def aggregate_kernel(
    own_ref, inner_ref, even_ref, odd_ref, theta_ref, theta_low_ref, phi_ref, phi_low_ref, cos_ref, sin_ref, pair_ref
):
    theta, theta_low = theta_ref[...], theta_low_ref[...]
    phi, phi_low = phi_ref[...], phi_low_ref[...]

    def narrow_of(box):
        ref, k = (own_ref, inner_ref)[box // 3], box % 3
        columns = []
        for x in range(2):
            parts = [ref[x, 64 * k : 64 * k + 64]]
            for rim_ref in (even_ref, odd_ref):
                parts += [rim_ref[x, r, pl.ds(8 * box, 8)] for r in range(2)]
            columns.append(jnp.concatenate(parts, axis=0))
        high, low = split(jnp.concatenate(columns, axis=1))
        return dot(theta, jnp.concatenate([high, low], axis=0)) + dot(theta_low, high)

    def wide_of(narrow):
        high, low = split(narrow)
        wide = []
        for x in range(2):
            part = slice(128 * x, 128 * x + 128)
            both = jnp.concatenate([high[:, part], low[:, part]], axis=1)
            wide.append(dot(both, phi) + dot(high[:, part], phi_low))
        return wide

    def store(box, wide):
        cosine, sine = cos_ref[...], sin_ref[...]
        real_part = (cosine * wide[0] - sine * wide[1]).reshape(8, 16, 256)
        imag_part = (cosine * wide[1] + sine * wide[0]).reshape(8, 16, 256)
        for x, value in enumerate((real_part, imag_part)):
            value = jnp.sum(value, axis=0)
            for half in range(2):
                rows = pl.ds(32 * box + 16 * half, 16)
                pair_ref[x, rows] = value[:, 128 * half : 128 * half + 128]

    narrow = [narrow_of(0), narrow_of(1)]
    wide = wide_of(narrow[0])
    for box in range(6):
        if box < 4:
            narrow.append(narrow_of(box + 2))
        ahead = wide_of(narrow[box + 1]) if box < 5 else None
        store(box, wide)
        wide = ahead


def aggregate(own, inner, even, odd, mats):
    return pl.pallas_call(
        aggregate_kernel,
        out_shape=jax.ShapeDtypeStruct((2, 192, 128), jnp.float32),
        in_specs=[spec(VMEM)] * 10,
        out_specs=spec(VMEM),
        compiler_params=PARAMS,
    )(own, inner, even, odd, *mats)


def fine_kernel(
    partner,
    offset,
    count,
    table,
    own,
    inner,
    outer,
    out,
    window,
    operators,
    value_ref,
    partner_ref,
    offset_ref,
    count_ref,
    sems,
    out_sems,
):
    me = lax.axis_index("box")
    odd = lax.rem(me, 2)
    moves = (
        (partner, partner_ref),
        (offset, offset_ref),
        (count, count_ref),
        (table, operators.at[:, pl.ds(0, 128)]),
        (own, window.at[:, pl.ds(192, 192)]),
        (inner, window.at[:, pl.ds(384 * (1 - odd), 192)]),
        (outer, window.at[:, pl.ds(384 * odd, 192)]),
    )
    copies = [pltpu.make_async_copy(*move, sems.at[i]) for i, move in enumerate(moves)]
    for copy in copies:
        copy.start()
    operators[:, 128:] = jnp.zeros((2, 8, 128), jnp.float32)
    for copy in copies:
        copy.wait()
    base = (me - 1) * 24

    def step(b, carry):
        sums = None
        for j in range(16):
            place = pl.multiple_of((partner_ref[j, b] - base) * 8, 8)
            which = pl.multiple_of(jnp.where(j < count_ref[b], offset_ref[j, b], 16) * 8, 8)
            a, c = operators[0, pl.ds(which, 8)], operators[1, pl.ds(which, 8)]
            f, g = window[0, pl.ds(place, 8)], window[1, pl.ds(place, 8)]
            terms = (a * f, c * g, a * g, c * f)
            sums = terms if sums is None else tuple(s + t for s, t in zip(sums, terms))
        value_ref[0, b] = sums[0] - sums[1]
        value_ref[1, b] = sums[2] + sums[3]
        return carry

    copies = []
    for part in range(3):
        lax.fori_loop(8 * part, 8 * part + 8, step, 0)
        boxes = pl.ds(8 * part, 8)
        copies.append(pltpu.make_async_copy(value_ref.at[:, boxes], out.at[:, boxes], out_sems.at[part]))
        copies[part].start()
    for copy in copies:
        copy.wait()


def in_hbm(*arrays):
    return tuple(pltpu.with_memory_space_constraint(x, pltpu.HBM) for x in arrays)


def fine_translate(pattern, inner, outer, table, partner, offset, count):
    return pl.pallas_call(
        fine_kernel,
        out_shape=jax.ShapeDtypeStruct((2, 24, 8, 128), jnp.float32),
        in_specs=[spec(pl.ANY)] * 7,
        out_specs=spec(pl.ANY),
        scratch_shapes=[
            pltpu.VMEM((2, 576, 128), jnp.float32),
            pltpu.VMEM((2, 136, 128), jnp.float32),
            pltpu.VMEM((2, 24, 8, 128), jnp.float32),
            pltpu.SMEM((16, 24), jnp.int32),
            pltpu.SMEM((16, 24), jnp.int32),
            pltpu.SMEM((24,), jnp.int32),
            pltpu.SemaphoreType.DMA((7,)),
            pltpu.SemaphoreType.DMA((3,)),
        ],
        compiler_params=PARAMS,
        cost_estimate=pl.CostEstimate(flops=4_000_000, bytes_accessed=4_000_000, transcendentals=0),
    )(*in_hbm(partner.T, offset.T, count, table.reshape(2, 128, 128)), pattern, inner, outer)


SIDE, SOURCES = 12, 21


def first_kernel(partner_ref, offset_ref, count_ref, table, pair_ref, out_ref, dense_ref):
    me = lax.axis_index("box")
    odd = lax.rem(me, 2) == 1
    base = (me // 2 - 2) * 6
    after = lax.rem(me // 2, 2) == lax.rem(me, 2)
    firsts = [jnp.where(odd, 18, 6), jnp.where(after, 12, 0), jnp.where(after, 0, 12), jnp.where(odd, 6, 18)]
    turns = [jnp.where(odd, 1, 0), jnp.where(odd == after, 0, 1), jnp.where(odd == after, 1, 0)]
    dense_ref[...] = jnp.zeros(dense_ref.shape, jnp.float32)

    def pick(box, values):
        before = jnp.where(box < 6, values[0], values[1])
        return jnp.where(box < 12, before, jnp.where(box < 24, values[2], values[3]))

    def step(b, carry):
        sums = [None, None]
        for j in range(16):
            live = j < count_ref[b]
            box, which = partner_ref[b, j] - base, offset_ref[b, j]
            here = jnp.logical_and(box >= 12, box < 18)
            place = box - jnp.where(here, 12, pick(box, (0, 6, 18, 24)))
            turned = jnp.where(here, turns[0], pick(box, (1, turns[1], turns[2], 0))) == 1
            place = jnp.where(turned, jnp.where(place < 3, place + 3, place - 3), place)
            away = jnp.logical_and(live, jnp.logical_not(here))
            entry = jnp.where(away, b * SOURCES + pick(box, firsts) + place, 3 * SOURCES)
            row = pl.multiple_of(entry * 16, 16)
            for x in range(2):
                dense_ref[x, pl.ds(row, 16)] = table[x, which]
            here = jnp.logical_and(live, here)
            place = pl.multiple_of(jnp.where(here, place, 0) * 32, 32)
            scale = jnp.where(here, 1.0, 0.0)
            for half in range(2):
                lanes = slice(128 * half, 128 * half + 128)
                rows = pl.ds(place + 16 * half, 16)
                a, c = table[0, which, :, lanes] * scale, table[1, which, :, lanes] * scale
                f, g = pair_ref[0, rows], pair_ref[1, rows]
                terms = (a * f, c * g, a * g, c * f)
                old = sums[half]
                sums[half] = terms if old is None else tuple(s + t for s, t in zip(old, terms))
        for half in range(2):
            lanes = slice(128 * half, 128 * half + 128)
            out_ref[0, b, :, lanes] = sums[half][0] - sums[half][1]
            out_ref[1, b, :, lanes] = sums[half][2] + sums[half][3]
        return carry

    lax.fori_loop(0, 3, step, 0)


def dense_sums(part, dense, sources, lines, lanes, half, top):
    sums = [(part[0, b, lines, lanes], part[1, b, lines, lanes]) for b in range(3)]
    for ref, row, entry in sources:
        rows = pl.ds(row + 16 * half + top, 8)
        f, g = ref[0, rows], ref[1, rows]
        for b in range(3):
            places = pl.ds((SOURCES * b + entry) * 16 + top, 8)
            a, c = dense[0, places, lanes], dense[1, places, lanes]
            sums[b] = (sums[b][0] + (a * f - c * g), sums[b][1] + (a * g + c * f))
    return sums


def second_kernel(next_ref, distant_ref, dense, part, out_ref):
    sources = [(next_ref, 32 * s, s) for s in range(6)] + [(distant_ref, 32 * s, 6 + s) for s in range(6)]
    for half in range(2):
        for top in (0, 8):
            lanes, lines = pl.ds(128 * half, 128), pl.ds(top, 8)
            sums = dense_sums(part, dense, sources, lines, lanes, half, top)
            for b in range(3):
                for x in range(2):
                    out_ref[x, b, lines, lanes] = sums[b][x]


def far_kernel(other, dense, part, out, value_ref, sems):
    sources = [(other, 32 * s, SIDE + s) for s in range(9)]
    copies = []
    for half in range(2):
        for top in (0, 8):
            lanes, lines = pl.ds(128 * half, 128), pl.ds(top, 8)
            sums = dense_sums(part, dense, sources, lines, lanes, half, top)
            for b in range(3):
                for x in range(2):
                    value_ref[x, b, lines, lanes] = sums[b][x]
            copies.append(
                pltpu.make_async_copy(
                    value_ref.at[:, :, lines, lanes], out.at[:, :, lines, lanes], sems.at[len(copies)]
                )
            )
            copies[-1].start()
    for copy in copies:
        copy.wait()


def first_translate(lists, table, pair):
    return pl.pallas_call(
        first_kernel,
        out_shape=(
            jax.ShapeDtypeStruct((2, 3, 16, 256), jnp.float32),
            jax.ShapeDtypeStruct((2, (3 * SOURCES + 1) * 16, 256), jnp.float32),
        ),
        in_specs=[spec(SMEM)] * 3 + [spec(VMEM)] * 2,
        out_specs=(spec(VMEM), spec(VMEM)),
        compiler_params=PARAMS,
    )(*lists, table, pair)


def second_translate(next_to, distant, dense, part):
    return pl.pallas_call(
        second_kernel,
        out_shape=jax.ShapeDtypeStruct((2, 3, 16, 256), jnp.float32),
        in_specs=[spec(VMEM)] * 4,
        out_specs=spec(VMEM),
        compiler_params=PARAMS,
    )(next_to, distant, dense, part)


def far_translate(other, dense, part):
    return pl.pallas_call(
        far_kernel,
        out_shape=jax.ShapeDtypeStruct((2, 3, 16, 256), jnp.float32),
        in_specs=[spec(VMEM)] * 3,
        out_specs=spec(pl.ANY),
        scratch_shapes=[pltpu.VMEM((2, 3, 16, 256), jnp.float32), pltpu.SemaphoreType.DMA((4,))],
        compiler_params=PARAMS,
    )(other, dense, part)


def shards(
    fine_pattern,
    fine_partner,
    fine_offset,
    fine_count,
    coarse_partner,
    coarse_offset,
    coarse_count,
    fine_table,
    coarse_table,
    theta_start,
    theta_weight,
    phi_interp,
    shift_phase,
):
    pattern = fine_pattern.reshape(2, 192, 128)
    inner = swap_cores(pattern)
    own, *mats = prepare(pattern, theta_start, theta_weight, phi_interp, shift_phase.reshape(128, 256))
    inner, own, mats = lax.optimization_barrier((inner, own, mats))
    even, odd = rims(own, inner)
    even, odd, late = lax.optimization_barrier((even, odd, own))
    outer = swap_chips(late, 1, 1)
    even, odd = swap_rims(even, 0), swap_rims(odd, 1)
    pair = aggregate(own, inner, even, odd, mats)
    next_to, distant = swap_next(pair), swap_chips(pair, 1, 2)
    fine_incoming = fine_translate(
        own, inner, outer, fine_table, fine_partner, fine_offset, fine_count
    )
    lists = (coarse_partner, coarse_offset, coarse_count)
    part, dense = first_translate(lists, coarse_table, pair)
    distant, fine_incoming, part, dense = lax.optimization_barrier((distant, fine_incoming, part, dense))
    next_to, distant = lax.optimization_barrier((next_to, distant))
    other = swap_cores(jnp.concatenate([next_to, distant[:, :96]], axis=1))
    part = second_translate(next_to, distant, dense, part)
    coarse_incoming = far_translate(other, dense, part)
    return (fine_incoming, coarse_incoming)


def solution(mesh):
    return jax.shard_map(
        shards,
        mesh=mesh,
        in_specs=(
            P(None, "box", "samp", None),
            P("box", None),
            P("box", None),
            P("box"),
            P("box", None),
            P("box", None),
            P("box"),
            P(None, None, "samp", None),
            P(None, None, "samp", None),
            P("samp"),
            P("samp", None),
            P(),
            P(None, "samp", None),
        ),
        out_specs=(P(None, "box", "samp", None), P(None, "box", "samp", None)),
        check_vma=False,
    )
```

```python
import functools

import jax
import jax.numpy as jnp
from jax import lax
from jax.experimental import pallas as pl
from jax.experimental.pallas import tpu as pltpu
from jax.sharding import PartitionSpec as P

VMEM = pltpu.VMEM
SMEM = pltpu.SMEM
PARAMS = pltpu.CompilerParams(vmem_limit_bytes=16 * 1024 * 1024)


def spec(space):
    return pl.BlockSpec(memory_space=space)


def matched(x, axis, pairs):
    return lax.ppermute(x, axis, pairs + [(j, i) for i, j in pairs])


def swap_cores(x):
    n = lax.axis_size("box")
    return matched(x, "box", [(i, i + 1) for i in range(0, n, 2)])


def swap_chips(x, core, distance):
    n = lax.axis_size("box")
    pairs = [(i + core, i + 2 * distance + 1 - core) for i in range(0, n - 2 * distance, 2)]
    return matched(x, "box", pairs)


def swap_next(x):
    n = lax.axis_size("box")
    return matched(x, "box", [(i, i + 2) for i in range(0, n - 2, 4)] + [(i, i + 2) for i in range(3, n - 2, 4)])


def swap_rims_across(x, start):
    n, m = lax.axis_size("box"), lax.axis_size("samp")
    pairs = [(i * m + z, (i ^ 1) * m + z + 1) for i in range(n) for z in range(start, m - 1, 2)]
    return matched(x, ("box", "samp"), pairs)


def swap_rims(x, start):
    n = lax.axis_size("samp")
    return matched(x, "samp", [(i, i + 1) for i in range(start, n - 1, 2)])


def rim_kernel(own_ref, inner_ref, even_ref, odd_ref):
    odd = lax.rem(lax.axis_index("samp"), 2) == 1
    for x in range(2):
        for row in range(2):
            for which, ref in enumerate((own_ref, inner_ref)):
                first = ref[x, pl.ds(row, 24, stride=8), :]
                last = ref[x, pl.ds(6 + row, 24, stride=8), :]
                boxes = pl.ds(24 * which, 24)
                even_ref[x, row, boxes] = jnp.where(odd, first, last)
                odd_ref[x, row, boxes] = jnp.where(odd, last, first)


def rims(own, inner):
    shape = jax.ShapeDtypeStruct((2, 2, 48, 128), jnp.float32)
    return pl.pallas_call(
        rim_kernel,
        out_shape=(shape, shape),
        in_specs=[spec(VMEM)] * 2,
        out_specs=(spec(VMEM), spec(VMEM)),
        compiler_params=PARAMS,
    )(own, inner)


def split(x):
    high = x.astype(jnp.bfloat16)
    return high, (x - high.astype(jnp.float32)).astype(jnp.bfloat16)


def dot(x, y):
    return jnp.dot(x, y, preferred_element_type=jnp.float32)


SINE = (-1 / 6, 1 / 120, -1 / 5040, 1 / 362880, -1 / 39916800, 1 / 6227020800)
COSINE = (-1 / 2, 1 / 24, -1 / 720, 1 / 40320, -1 / 3628800, 1 / 479001600)


def series(square, terms):
    total = square * terms[-1]
    for term in terms[-2::-1]:
        total = square * (total + term)
    return total + 1.0


def prepare_kernel(
    start,
    weight,
    pattern,
    phi,
    phase,
    own_ref,
    theta_ref,
    theta_low_ref,
    phi_out_ref,
    phi_low_ref,
    cos_ref,
    sin_ref,
    phi_ref,
    start_ref,
    weight_ref,
    sems,
):
    copies = [
        pltpu.make_async_copy(phi, phi_ref, sems.at[0]),
        pltpu.make_async_copy(phase, sin_ref, sems.at[1]),
        pltpu.make_async_copy(pattern, own_ref, sems.at[2]),
        pltpu.make_async_copy(start, start_ref, sems.at[3]),
        pltpu.make_async_copy(weight, weight_ref, sems.at[4]),
    ]
    for copy in copies[3:] + copies[:3]:
        copy.start()
    copies[3].wait()
    copies[4].wait()
    samp = lax.axis_index("samp")
    line = lax.broadcasted_iota(jnp.int32, (16, 96), 0)
    column = lax.broadcasted_iota(jnp.int32, (16, 96), 1)
    rim = (column - 64) // 8
    rim = jnp.where((rim < 2) == (lax.rem(samp, 2) == 1), rim % 2 - 2, rim % 2 + 8)
    row = jnp.where(column < 64, column % 8, rim) + samp * 8
    theta = jnp.zeros((16, 96), jnp.float32)
    for i in range(16):
        for q in range(4):
            theta = theta + jnp.where((row == start_ref[i] + q) & (line == i), weight_ref[q, i], 0.0)
    theta = jnp.concatenate([theta] * 8, axis=0)
    line = lax.broadcasted_iota(jnp.int32, (128, 96), 0)
    column = lax.broadcasted_iota(jnp.int32, (128, 96), 1)
    child = jnp.where(column < 64, column // 8, column % 8)
    theta = jnp.where(child == line // 16, theta, 0.0)
    high, low = split(theta)
    theta_ref[...] = jnp.concatenate([high, high], axis=1)
    theta_low_ref[...] = low
    copies[0].wait()
    high, low = split(phi_ref[...].T)
    phi_out_ref[...] = jnp.concatenate([high, high], axis=0)
    phi_low_ref[...] = low
    copies[1].wait()
    half = sin_ref[...] * 0.5
    square = half * half
    sine = half * series(square, SINE)
    cos_ref[...] = 1.0 - 2.0 * sine * sine
    sin_ref[...] = 2.0 * sine * series(square, COSINE)
    copies[2].wait()


def prepare(pattern, start, weight, phi, phase):
    half, full = jnp.bfloat16, jnp.float32
    shapes = (
        ((2, 192, 128), full),
        ((128, 192), half),
        ((128, 96), half),
        ((256, 256), half),
        ((128, 256), half),
        ((128, 256), full),
        ((128, 256), full),
    )
    return pl.pallas_call(
        prepare_kernel,
        out_shape=tuple(jax.ShapeDtypeStruct(*s) for s in shapes),
        in_specs=[spec(pl.ANY)] * 5,
        out_specs=(spec(VMEM),) * 7,
        scratch_shapes=[
            pltpu.VMEM((256, 128), jnp.float32),
            pltpu.SMEM((16,), jnp.int32),
            pltpu.SMEM((4, 16), jnp.float32),
            pltpu.SemaphoreType.DMA((5,)),
        ],
        compiler_params=PARAMS,
    )(*in_hbm(start, weight.T, pattern, phi, phase))


def aggregate_kernel(
    own_ref, inner_ref, even_ref, odd_ref, theta_ref, theta_low_ref, phi_ref, phi_low_ref, cos_ref, sin_ref, pair_ref
):
    theta, theta_low = theta_ref[...], theta_low_ref[...]
    phi, phi_low = phi_ref[...], phi_low_ref[...]

    def narrow_of(box):
        ref, k = (own_ref, inner_ref)[box // 3], box % 3
        columns = []
        for x in range(2):
            parts = [ref[x, 64 * k : 64 * k + 64]]
            for rim_ref, first in ((even_ref, 8 * box), (odd_ref, 8 * ((box + 3) % 6))):
                parts += [rim_ref[x, r, pl.ds(first, 8)] for r in range(2)]
            columns.append(jnp.concatenate(parts, axis=0))
        high, low = split(jnp.concatenate(columns, axis=1))
        return dot(theta, jnp.concatenate([high, low], axis=0)) + dot(theta_low, high)

    def wide_of(narrow):
        high, low = split(narrow)
        wide = []
        for x in range(2):
            part = slice(128 * x, 128 * x + 128)
            both = jnp.concatenate([high[:, part], low[:, part]], axis=1)
            wide.append(dot(both, phi) + dot(high[:, part], phi_low))
        return wide

    def store(box, wide):
        cosine, sine = cos_ref[...], sin_ref[...]
        real_part = (cosine * wide[0] - sine * wide[1]).reshape(8, 16, 256)
        imag_part = (cosine * wide[1] + sine * wide[0]).reshape(8, 16, 256)
        for x, value in enumerate((real_part, imag_part)):
            value = jnp.sum(value, axis=0)
            for half in range(2):
                rows = pl.ds(32 * box + 16 * half, 16)
                pair_ref[x, rows] = value[:, 128 * half : 128 * half + 128]

    narrow = [narrow_of(0), narrow_of(1)]
    wide = wide_of(narrow[0])
    for box in range(6):
        if box < 4:
            narrow.append(narrow_of(box + 2))
        ahead = wide_of(narrow[box + 1]) if box < 5 else None
        store(box, wide)
        wide = ahead


def aggregate(own, inner, even, odd, mats):
    return pl.pallas_call(
        aggregate_kernel,
        out_shape=jax.ShapeDtypeStruct((2, 192, 128), jnp.float32),
        in_specs=[spec(VMEM)] * 10,
        out_specs=spec(VMEM),
        compiler_params=PARAMS,
    )(own, inner, even, odd, *mats)


def fine_kernel(
    partner,
    offset,
    count,
    table,
    own,
    inner,
    outer,
    out,
    window,
    operators,
    value_ref,
    partner_ref,
    offset_ref,
    count_ref,
    sems,
    out_sems,
):
    me = lax.axis_index("box")
    odd = lax.rem(me, 2)
    moves = (
        (partner, partner_ref),
        (offset, offset_ref),
        (count, count_ref),
        (table, operators.at[:, pl.ds(0, 128)]),
        (own, window.at[:, pl.ds(192, 192)]),
        (inner, window.at[:, pl.ds(384 * (1 - odd), 192)]),
        (outer, window.at[:, pl.ds(384 * odd, 192)]),
    )
    copies = [pltpu.make_async_copy(*move, sems.at[i]) for i, move in enumerate(moves)]
    for copy in copies:
        copy.start()
    operators[:, 128:] = jnp.zeros((2, 8, 128), jnp.float32)
    for copy in copies:
        copy.wait()
    base = (me - 1) * 24

    def step(b, carry):
        sums = None
        for j in range(16):
            place = pl.multiple_of((partner_ref[j, b] - base) * 8, 8)
            which = pl.multiple_of(jnp.where(j < count_ref[b], offset_ref[j, b], 16) * 8, 8)
            a, c = operators[0, pl.ds(which, 8)], operators[1, pl.ds(which, 8)]
            f, g = window[0, pl.ds(place, 8)], window[1, pl.ds(place, 8)]
            terms = (a * f, c * g, a * g, c * f)
            sums = terms if sums is None else tuple(s + t for s, t in zip(sums, terms))
        value_ref[0, b] = sums[0] - sums[1]
        value_ref[1, b] = sums[2] + sums[3]
        return carry

    copies = []
    for part in range(3):
        lax.fori_loop(8 * part, 8 * part + 8, step, 0)
        boxes = pl.ds(8 * part, 8)
        copies.append(pltpu.make_async_copy(value_ref.at[:, boxes], out.at[:, boxes], out_sems.at[part]))
        copies[part].start()
    for copy in copies:
        copy.wait()


def in_hbm(*arrays):
    return tuple(pltpu.with_memory_space_constraint(x, pltpu.HBM) for x in arrays)


def fine_translate(pattern, inner, outer, table, partner, offset, count):
    return pl.pallas_call(
        fine_kernel,
        out_shape=jax.ShapeDtypeStruct((2, 24, 8, 128), jnp.float32),
        in_specs=[spec(pl.ANY)] * 7,
        out_specs=spec(pl.ANY),
        scratch_shapes=[
            pltpu.VMEM((2, 576, 128), jnp.float32),
            pltpu.VMEM((2, 136, 128), jnp.float32),
            pltpu.VMEM((2, 24, 8, 128), jnp.float32),
            pltpu.SMEM((16, 24), jnp.int32),
            pltpu.SMEM((16, 24), jnp.int32),
            pltpu.SMEM((24,), jnp.int32),
            pltpu.SemaphoreType.DMA((7,)),
            pltpu.SemaphoreType.DMA((3,)),
        ],
        compiler_params=PARAMS,
        cost_estimate=pl.CostEstimate(flops=4_000_000, bytes_accessed=4_000_000, transcendentals=0),
    )(*in_hbm(partner.T, offset.T, count, table.reshape(2, 128, 128)), pattern, inner, outer)


SIDE, SOURCES = 12, 21


def first_kernel(partner_ref, offset_ref, count_ref, table, pair_ref, out_ref, dense_ref):
    me = lax.axis_index("box")
    odd = lax.rem(me, 2) == 1
    base = (me // 2 - 2) * 6
    after = lax.rem(me // 2, 2) == lax.rem(me, 2)
    firsts = [jnp.where(odd, 18, 6), jnp.where(after, 12, 0), jnp.where(after, 0, 12), jnp.where(odd, 6, 18)]
    turns = [jnp.where(odd, 1, 0), jnp.where(odd == after, 0, 1), jnp.where(odd == after, 1, 0)]
    dense_ref[...] = jnp.zeros(dense_ref.shape, jnp.float32)

    def pick(box, values):
        before = jnp.where(box < 6, values[0], values[1])
        return jnp.where(box < 12, before, jnp.where(box < 24, values[2], values[3]))

    def step(b, carry):
        sums = [None, None]
        for j in range(16):
            live = j < count_ref[b]
            box, which = partner_ref[b, j] - base, offset_ref[b, j]
            here = jnp.logical_and(box >= 12, box < 18)
            place = box - jnp.where(here, 12, pick(box, (0, 6, 18, 24)))
            turned = jnp.where(here, turns[0], pick(box, (1, turns[1], turns[2], 0))) == 1
            place = jnp.where(turned, jnp.where(place < 3, place + 3, place - 3), place)
            away = jnp.logical_and(live, jnp.logical_not(here))
            entry = jnp.where(away, b * SOURCES + pick(box, firsts) + place, 3 * SOURCES)
            row = pl.multiple_of(entry * 16, 16)
            for x in range(2):
                dense_ref[x, pl.ds(row, 16)] = table[x, which]
            here = jnp.logical_and(live, here)
            place = pl.multiple_of(jnp.where(here, place, 0) * 32, 32)
            scale = jnp.where(here, 1.0, 0.0)
            for half in range(2):
                lanes = slice(128 * half, 128 * half + 128)
                rows = pl.ds(place + 16 * half, 16)
                a, c = table[0, which, :, lanes] * scale, table[1, which, :, lanes] * scale
                f, g = pair_ref[0, rows], pair_ref[1, rows]
                terms = (a * f, c * g, a * g, c * f)
                old = sums[half]
                sums[half] = terms if old is None else tuple(s + t for s, t in zip(old, terms))
        for half in range(2):
            lanes = slice(128 * half, 128 * half + 128)
            out_ref[0, b, :, lanes] = sums[half][0] - sums[half][1]
            out_ref[1, b, :, lanes] = sums[half][2] + sums[half][3]
        return carry

    lax.fori_loop(0, 3, step, 0)


def dense_sums(part, dense, sources, lines, lanes, half, top):
    sums = [(part[0, b, lines, lanes], part[1, b, lines, lanes]) for b in range(3)]
    for ref, row, entry in sources:
        rows = pl.ds(row + 16 * half + top, 8)
        f, g = ref[0, rows], ref[1, rows]
        for b in range(3):
            places = pl.ds((SOURCES * b + entry) * 16 + top, 8)
            a, c = dense[0, places, lanes], dense[1, places, lanes]
            sums[b] = (sums[b][0] + (a * f - c * g), sums[b][1] + (a * g + c * f))
    return sums


def second_kernel(next_ref, distant_ref, dense, part, out_ref):
    sources = [(next_ref, 32 * s, s) for s in range(6)] + [(distant_ref, 32 * s, 6 + s) for s in range(6)]
    for half in range(2):
        for top in (0, 8):
            lanes, lines = pl.ds(128 * half, 128), pl.ds(top, 8)
            sums = dense_sums(part, dense, sources, lines, lanes, half, top)
            for b in range(3):
                for x in range(2):
                    out_ref[x, b, lines, lanes] = sums[b][x]


def far_kernel(other, dense, part, out, value_ref, sems):
    sources = [(other, 32 * s, SIDE + s) for s in range(9)]
    copies = []
    for half in range(2):
        for top in (0, 8):
            lanes, lines = pl.ds(128 * half, 128), pl.ds(top, 8)
            sums = dense_sums(part, dense, sources, lines, lanes, half, top)
            for b in range(3):
                for x in range(2):
                    value_ref[x, b, lines, lanes] = sums[b][x]
            copies.append(
                pltpu.make_async_copy(
                    value_ref.at[:, :, lines, lanes], out.at[:, :, lines, lanes], sems.at[len(copies)]
                )
            )
            copies[-1].start()
    for copy in copies:
        copy.wait()


def first_translate(lists, table, pair):
    return pl.pallas_call(
        first_kernel,
        out_shape=(
            jax.ShapeDtypeStruct((2, 3, 16, 256), jnp.float32),
            jax.ShapeDtypeStruct((2, (3 * SOURCES + 1) * 16, 256), jnp.float32),
        ),
        in_specs=[spec(SMEM)] * 3 + [spec(VMEM)] * 2,
        out_specs=(spec(VMEM), spec(VMEM)),
        compiler_params=PARAMS,
    )(*lists, table, pair)


def second_translate(next_to, distant, dense, part):
    return pl.pallas_call(
        second_kernel,
        out_shape=jax.ShapeDtypeStruct((2, 3, 16, 256), jnp.float32),
        in_specs=[spec(VMEM)] * 4,
        out_specs=spec(VMEM),
        compiler_params=PARAMS,
    )(next_to, distant, dense, part)


def far_translate(other, dense, part):
    return pl.pallas_call(
        far_kernel,
        out_shape=jax.ShapeDtypeStruct((2, 3, 16, 256), jnp.float32),
        in_specs=[spec(VMEM)] * 3,
        out_specs=spec(pl.ANY),
        scratch_shapes=[pltpu.VMEM((2, 3, 16, 256), jnp.float32), pltpu.SemaphoreType.DMA((4,))],
        compiler_params=PARAMS,
    )(other, dense, part)


def shards(
    fine_pattern,
    fine_partner,
    fine_offset,
    fine_count,
    coarse_partner,
    coarse_offset,
    coarse_count,
    fine_table,
    coarse_table,
    theta_start,
    theta_weight,
    phi_interp,
    shift_phase,
):
    pattern = fine_pattern.reshape(2, 192, 128)
    inner = swap_cores(pattern)
    own, *mats = prepare(pattern, theta_start, theta_weight, phi_interp, shift_phase.reshape(128, 256))
    inner, own, mats = lax.optimization_barrier((inner, own, mats))
    even, odd = rims(own, inner)
    even, odd, late = lax.optimization_barrier((even, odd, own))
    outer = swap_chips(late, 1, 1)
    even, odd = swap_rims(even, 0), swap_rims_across(odd, 1)
    pair = aggregate(own, inner, even, odd, mats)
    next_to, distant = swap_next(pair), swap_chips(pair, 1, 2)
    fine_incoming = fine_translate(
        own, inner, outer, fine_table, fine_partner, fine_offset, fine_count
    )
    lists = (coarse_partner, coarse_offset, coarse_count)
    part, dense = first_translate(lists, coarse_table, pair)
    distant, fine_incoming, part, dense = lax.optimization_barrier((distant, fine_incoming, part, dense))
    next_to, distant = lax.optimization_barrier((next_to, distant))
    other = swap_cores(jnp.concatenate([next_to, distant[:, :96]], axis=1))
    part = second_translate(next_to, distant, dense, part)
    coarse_incoming = far_translate(other, dense, part)
    return (fine_incoming, coarse_incoming)


def solution(mesh):
    return jax.shard_map(
        shards,
        mesh=mesh,
        in_specs=(
            P(None, "box", "samp", None),
            P("box", None),
            P("box", None),
            P("box"),
            P("box", None),
            P("box", None),
            P("box"),
            P(None, None, "samp", None),
            P(None, None, "samp", None),
            P("samp"),
            P("samp", None),
            P(),
            P(None, "samp", None),
        ),
        out_specs=(P(None, "box", "samp", None), P(None, "box", "samp", None)),
        check_vma=False,
    )
```
